32 devices in a mesh: group: 2 (over x), tm: 8 (over z, y), space: 2 (over core).
Axes of the slice: x: 2, y: 2, z: 4, core: 2. Of those that a mesh axis runs over, the one named last changes fastest.
Arguments:
- right_side: float32 [16, 2, 32, 64, 128], P(('group', 'tm'), None, 'space'), parts along dimension 0, may hold values from -6 to 6
- diffusivity: float32 [32, 64, 128], P('space'), may hold values from 0.05 to 0.5
- velocity: float32 [3, 32, 64, 128], P(None, 'space'), may hold values from -0.5 to 0.5
Outputs:
- solution: float32 [16, 2, 32, 64, 128], P(('group', 'tm'), None, 'space'), parts along dimension 0
The draws below stay inside these ranges and needn't reach their ends.
There are 2 independent parts, one for each index of `group`. The reference program is written for one: setup_inputs(seed, part) draws one part's arguments, and reference() takes and returns one part's arrays. A program takes and returns all parts, laid end to end along the dimension named above; an argument that names none is the same for every part. Nothing has to cross between parts.
All inputs are finite; a program needn't handle non-finite values.
Results may differ from the reference program's by a relative error of at most 0.0003.
Values sent between devices are 32-bit elements; how exact they have to be, the bound alone decides.
No kernel may reach another device: no remote copies, remote signals or barrier semaphores. Data moves between devices by JAX's collectives and lax.ppermute only.
A program may use at most 64 MiB of HBM per device.

```python
import math
import jax
import jax.numpy as jnp

NX = 64
NY = 128
SWEEPS = 4
TSTEPS = 8
NZ = 32


def steps_of(own_key, shape, shards, low, largest):
    def one(axis_at, blocks):
        draws = jax.random.uniform(jax.random.fold_in(jax.random.fold_in(own_key, 6), axis_at), (blocks,), jnp.float32, low / len(shards), largest / len(shards))
        return jnp.repeat(jnp.exp(draws), shape[axis_at] // blocks).reshape((-1,) + (1,) * (len(shape) - axis_at - 1))

    factor_of = one(*shards[0])
    for cut in shards[1:]:
        factor_of = factor_of * one(*cut)
    return factor_of


def bell_draw(stream_key, extent, scale, bound, shards=(), kind=jnp.bfloat16):
    values = scale * jax.random.normal(stream_key, extent, jnp.float32)
    if shards:
        values = values * steps_of(stream_key, extent, shards, -0.22, 0.18)
    return jnp.clip(values, -bound, bound).astype(kind)


def setup_inputs(seed: int = 0, part: int = 0) -> dict:
    splits = jax.random.split(jax.random.key(seed), 4)
    part_splits = jax.random.split(jax.random.fold_in(splits[3], part), 4)
    return {
        "right_side": bell_draw(part_splits[0], (TSTEPS, 2, NZ, NX, NY), 1.0, 6.0, ((0, 8), (2, 2)), jnp.float32),
        "diffusivity": jnp.clip(jnp.exp(math.log(0.5) - 2.3025851 * jax.random.uniform(splits[1], (NZ, NX, NY), jnp.float32) ** steps_of(splits[1], (NZ, NX, NY), ((0, 2),), -0.2, 0.2)), 0.05, 0.5),
        "velocity": jnp.clip(jax.random.uniform(splits[2], (3, NZ, NX, NY), jnp.float32, -0.5, 0.5) * steps_of(splits[2], (3, NZ, NX, NY), ((1, 2),), -0.4, 0.0), -0.5, 0.5),
    }


alpha_circ = 0.1
inv_step = 2.0


def couple(padded, diffusivity, forward_flow, backward_flow):
    below_z = padded[..., :-2, 1:-1, 1:-1]
    above_z = padded[..., 2:, 1:-1, 1:-1]
    below_x = padded[..., 1:-1, :-2, 1:-1]
    above_x = padded[..., 1:-1, 2:, 1:-1]
    below_y = padded[..., 1:-1, 1:-1, :-2]
    above_y = padded[..., 1:-1, 1:-1, 2:]
    combined = diffusivity * (below_z + above_z + below_x + above_x + below_y + above_y)
    combined = combined + forward_flow[0] * below_z + backward_flow[0] * above_z
    combined = combined + forward_flow[1] * below_x + backward_flow[1] * above_x
    combined = combined + forward_flow[2] * below_y + backward_flow[2] * above_y
    return combined


def inverse_diagonal(diffusivity, velocity, lam_re, lam_im):
    real_part = lam_re + 6.0 * diffusivity + jnp.sum(jnp.abs(velocity), axis=0)
    magnitude = real_part * real_part + lam_im * lam_im
    return real_part / magnitude, -lam_im / magnitude


def rotate(real_part, imag_part, cos_part, sin_part):
    return real_part * cos_part - imag_part * sin_part, real_part * sin_part + imag_part * cos_part


def jacobi_step(source, nearby, inv_real, inv_imag):
    combined = source + nearby
    new_real, new_imag = rotate(combined[:, 0], combined[:, 1], inv_real, inv_imag)
    return jnp.stack([new_real, new_imag], axis=1)


def reference(right_side, diffusivity, velocity):
    step_float = jnp.arange(TSTEPS).astype(jnp.float32)
    log_alpha = jnp.log(jnp.float32(alpha_circ))
    weights = jnp.exp(step_float / TSTEPS * log_alpha)
    grid_field = (right_side[:, 0] + 1j * right_side[:, 1]) * weights[:, None, None, None]
    spectrum = jnp.fft.fft(grid_field, axis=0)
    phase_angle = (2.0 * jnp.pi / TSTEPS) * step_float
    radius = jnp.exp(log_alpha / TSTEPS)
    lam_re = (inv_step * (1.0 - radius * jnp.cos(phase_angle)))[:, None, None, None]
    lam_im = (inv_step * radius * jnp.sin(phase_angle))[:, None, None, None]
    inv_real, inv_imag = inverse_diagonal(diffusivity, velocity, lam_re, lam_im)
    forward_flow = jnp.maximum(velocity, 0.0)
    backward_flow = jnp.maximum(-velocity, 0.0)
    source = jnp.stack([jnp.real(spectrum), jnp.imag(spectrum)], axis=1).astype(jnp.float32)
    iterate = jnp.zeros_like(source)
    for sweep_number in range(SWEEPS):
        padded = jnp.pad(iterate, ((0, 0), (0, 0), (1, 1), (1, 1), (1, 1)))
        iterate = jacobi_step(source, couple(padded, diffusivity, forward_flow, backward_flow), inv_real, inv_imag)
    solved = iterate[:, 0] + 1j * iterate[:, 1]
    restored = jnp.fft.ifft(solved, axis=0) / weights[:, None, None, None]
    return jnp.stack([jnp.real(restored), jnp.imag(restored)], axis=1).astype(jnp.float32)
```

```python
import functools

import jax
import jax.numpy as jnp
from jax import lax
from jax.experimental import pallas as pl
from jax.experimental.pallas import tpu as pltpu
from jax.sharding import PartitionSpec as P

SWEEPS = 4
GHOST = SWEEPS - 1
QUARTERS = 4
TILE = 8
COEFS = 9

alpha_circ = 0.1
inv_step = 2.0

FLAT = ("tm", "space")


class Plan:
    def __init__(self, steps, cores, half_z, nx, ny):
        self.steps, self.cores, self.half_z, self.nx, self.ny = steps, cores, half_z, nx, ny
        self.z_parts = steps // QUARTERS
        self.in_half = self.z_parts // cores
        self.nz = half_z // self.in_half
        self.rows = nx // QUARTERS
        self.main = self.rows // TILE
        self.tiles = self.main + 1
        self.ext = self.nz + 2 * GHOST
        order = [2, 3, 1, 0]
        self.rounds = [(a, m, c) for a in order for m in range(self.in_half) for c in range(2)]

    def flat(self, hi, zb, s):
        return (hi * self.z_parts + zb) * self.cores + s

    def pairs(self, a, m, c):
        result = []
        for hi in range(QUARTERS):
            for jm in range(self.in_half):
                for jb in range(2):
                    for h in range(self.cores):
                        source = self.flat(hi, jm * 2 + jb, h)
                        target = self.flat(hi ^ a, h * self.in_half + (jm ^ m), jb ^ c)
                        result.append((source, target))
        return result

    def x_pairs(self, first):
        result = []
        for hi in range(first, QUARTERS - 1, 2):
            for zb in range(self.z_parts):
                for s in range(self.cores):
                    one, two = self.flat(hi, zb, s), self.flat(hi + 1, zb, s)
                    result += [(one, two), (two, one)]
        return result

    def z_pairs(self, first):
        result = []
        for zb in range(first, self.z_parts - 1, 2):
            for hi in range(QUARTERS):
                for s in range(self.cores):
                    one, two = self.flat(hi, zb, s), self.flat(hi, zb + 1, s)
                    result += [(one, two), (two, one)]
        return result

    def time_of(self, hi, zb, s, a, m, c):
        return ((hi ^ a) * self.in_half + ((zb % self.in_half) ^ m)) * 2 + (s ^ c)


def kernel_call(body, outs, args, scalars=True, scratch=(), cost=None):
    in_specs = [pl.BlockSpec(memory_space=pltpu.VMEM)] * len(args)
    if scalars:
        in_specs[0] = pl.BlockSpec(memory_space=pltpu.SMEM)
    single = isinstance(outs, tuple)
    shapes = [outs] if single else list(outs)
    result = pl.pallas_call(
        body,
        out_shape=[jax.ShapeDtypeStruct(s, jnp.float32) for s in shapes],
        in_specs=in_specs,
        out_specs=[pl.BlockSpec(memory_space=pltpu.VMEM)] * len(shapes),
        scratch_shapes=list(scratch),
        compiler_params=pltpu.CompilerParams(vmem_limit_bytes=40 << 20),
    )(*args)
    return result[0] if single else result


def rows_at(index, count=1):
    return pl.ds(pl.multiple_of(index * TILE, TILE), count * TILE)


def sublane(plan):
    return lax.broadcasted_iota(jnp.int32, (TILE, plan.ny), 0)


def lane(plan):
    return lax.broadcasted_iota(jnp.int32, (TILE, plan.ny), 1)


def pack_coefs(plan, place, d_ref, v_ref, out_ref):
    hi = place[0]
    per = plan.nx // TILE
    below = jnp.maximum(hi * plan.main - 1, 0)
    above = jnp.minimum(hi * plan.main + plan.main, per - 1)
    row = sublane(plan)

    def layer(z, _):
        for n in range(4):
            ref, base = (d_ref, z * per) if n == 0 else (v_ref, ((n - 1) * plan.half_z + z) * per)
            at = (n * plan.half_z + z) * plan.tiles
            for k in range(plan.main):
                out_ref[rows_at(at + k), :] = ref[rows_at(base + hi * plan.main + k), :]
            over, under = ref[rows_at(base + above), :], ref[rows_at(base + below), :]
            edge = jnp.where(row < TILE // 2, over, under)
            out_ref[rows_at(at + plan.main), :] = edge
        return 0

    lax.fori_loop(0, plan.half_z, layer, 0)


def make_coefs(plan, place, own_ref, other_ref, out_ref):
    hi, zb, s = place[0], place[1], place[2]
    row, col = sublane(plan), lane(plan)

    def layer(e, _):
        depth = zb * plan.nz + e - GHOST
        inside = (depth >= 0) & (depth < plan.half_z * plan.cores)
        depth = jnp.clip(depth, 0, plan.half_z * plan.cores - 1)
        mine = depth // plan.half_z == s
        z = depth % plan.half_z
        for k in range(plan.tiles):
            values = []
            for n in range(4):
                at = rows_at((n * plan.half_z + z) * plan.tiles + k)
                values.append(jnp.where(mine, own_ref[at, :], other_ref[at, :]))
            d, vz, vx, vy = values
            if k < plan.main:
                x = row + k * TILE
            else:
                x = jnp.where(row < GHOST, row + plan.rows, row - TILE)
            x = x + hi * plan.rows
            keep = (x >= 0) & (x < plan.nx) & inside
            if k == plan.main:
                keep = keep & ((row < GHOST) | (row >= TILE - GHOST))
            total = inv_step + 6.0 * d + (jnp.abs(vz) + jnp.abs(vx) + jnp.abs(vy))
            w = jnp.where(keep, 1.0 / total, 0.0)
            c = inv_step * w
            power = c
            for _ in range(plan.steps.bit_length() - 1):
                power = power * power
            wrap = alpha_circ / (1.0 - alpha_circ * power)
            low = [w * (d + jnp.maximum(v, 0.0)) for v in (vz, vx, vy)]
            high = [w * (d + jnp.maximum(-v, 0.0)) for v in (vz, vx, vy)]
            low[2] = jnp.where(col == 0, 0.0, low[2])
            high[2] = jnp.where(col == plan.ny - 1, 0.0, high[2])
            made = [w, c, wrap] + low + high
            for n, value in enumerate(made):
                out_ref[rows_at((e * plan.tiles + k) * COEFS + n), :] = value
        return 0

    lax.fori_loop(0, plan.ext, layer, 0)


def gather_steps(plan, place, *refs):
    hi, zb, s = place[0], place[1], place[2]
    blocks, (field, x_even, x_odd, *z_sends) = refs[: plan.steps], refs[plan.steps :]
    size = plan.nz * plan.rows
    hi_odd = hi % 2 == 1
    zb_odd = zb % 2 == 1
    for block, (a, m, c) in zip(blocks, plan.rounds):
        step = plan.time_of(hi, zb, s, a, m, c)
        field[pl.ds(pl.multiple_of(step * size, TILE), size), :] = block[...]
        for r in range(GHOST):
            low = block[pl.ds(r, plan.nz, stride=plan.rows), :]
            high = block[pl.ds(plan.rows - GHOST + r, plan.nz, stride=plan.rows), :]
            at = pl.ds(r * plan.steps * plan.nz + step * plan.nz, plan.nz)
            x_even[at, :] = jnp.where(hi_odd, low, high)
            x_odd[at, :] = jnp.where(hi_odd, high, low)
        edge = GHOST * plan.rows
        at = pl.ds(pl.multiple_of(step * edge, TILE), edge)
        low, high = block[:edge, :], block[size - edge :, :]
        for first, z_send in enumerate(z_sends):
            z_send[at, :] = jnp.where(zb_odd ^ (first == 1), low, high)


def gather_ghosts(plan, place, even_ref, odd_ref, planes, *corners):
    hi, zb = place[0], place[1]
    hi_odd = hi % 2 == 1
    zb_odd = zb % 2 == 1
    count = plan.steps * plan.nz
    for r in range(GHOST):
        even, odd = even_ref[pl.ds(r * count, count), :], odd_ref[pl.ds(r * count, count), :]
        planes[pl.ds(r * count, count), :] = jnp.where(hi_odd, odd, even)
        planes[pl.ds((TILE - GHOST + r) * count, count), :] = jnp.where(hi_odd, even, odd)
    for r in range(GHOST, TILE - GHOST):
        planes[pl.ds(r * count, count), :] = jnp.zeros((count, plan.ny), jnp.float32)
    deep = GHOST - 1
    for step in range(plan.steps):
        for n in range(deep):
            low = planes[pl.ds(step * plan.nz + n, TILE, stride=count), :]
            high = planes[pl.ds(step * plan.nz + plan.nz - deep + n, TILE, stride=count), :]
            for first, corner in enumerate(corners):
                corner[rows_at(step * deep + n), :] = jnp.where(zb_odd ^ (first == 1), low, high)


def sweep_kernel(plan, place, coefs, field, planes, *refs):
    hi, zb, s = place[0], place[1], place[2]
    sides = 1 if plan.z_parts == 2 else 2
    z_in, refs = refs[:sides], refs[sides:]
    c_in, refs = refs[:sides], refs[sides:]
    outs, (source, ping, pong, last) = refs[: plan.steps], refs[plan.steps :]
    steps, tiles, main, ny = plan.steps, plan.tiles, plan.main, plan.ny
    count = steps * plan.nz
    deep = GHOST - 1
    zb_odd = zb % 2 == 1
    row = sublane(plan)
    has_low, has_high = zb > 0, zb < plan.z_parts - 1

    def spot(e, k, t):
        return rows_at((e * tiles + k) * steps + t)

    def coef(e, k, n):
        return coefs[rows_at((e * tiles + k) * COEFS + n), :]

    def solve(c, wrap, scaled):
        partial = [scaled[0]]
        for value in scaled[1:]:
            partial.append(value + c * partial[-1])
        carry = c * (wrap * partial[-1])
        result = []
        for value in partial:
            result.append(value + carry)
            carry = c * carry
        return result

    def first(e, k, values):
        w, c, wrap = (coef(e, k, n) for n in range(3))
        scaled = [w * value for value in values]
        for t, (value, solved) in enumerate(zip(scaled, solve(c, wrap, scaled))):
            source[spot(e, k, t), :] = value
            ping[spot(e, k, t), :] = solved

    def own_layer(z, _):
        e = z + GHOST
        for k in range(main):
            first(e, k, [field[rows_at((t * plan.nz + z) * main + k), :] for t in range(steps)])
        first(e, main, [planes[pl.ds(t * plan.nz + z, TILE, stride=count), :] for t in range(steps)])
        return 0

    lax.fori_loop(0, plan.nz, own_layer, 0)

    empty = jnp.zeros((TILE, ny), jnp.float32)

    def ghost_layers(at, upper, main_ref, corner_ref):
        for n in range(GHOST):
            e = at + n
            for k in range(main):
                first(e, k, [main_ref[rows_at((t * GHOST + n) * main + k), :] for t in range(steps)])
            c_at = n if upper else n - (GHOST - deep)
            if 0 <= c_at < deep:
                first(e, main, [corner_ref[rows_at(t * deep + c_at), :] for t in range(steps)])
            else:
                for t in range(steps):
                    ping[spot(e, main, t), :] = empty
                    source[spot(e, main, t), :] = empty

    def no_layer(e):
        for k in range(tiles):
            for t in range(steps):
                ping[spot(e, k, t), :] = empty
                pong[spot(e, k, t), :] = empty

    high_at = GHOST + plan.nz
    for odd in (False, True):

        @pl.when(has_low & (zb_odd == odd))
        def _():
            pick = 0 if odd else sides - 1
            ghost_layers(0, False, z_in[pick], c_in[pick])

        @pl.when(has_high & (zb_odd == odd))
        def _():
            pick = sides - 1 if odd else 0
            ghost_layers(high_at, True, z_in[pick], c_in[pick])

    @pl.when(jnp.logical_not(has_low))
    def _():
        no_layer(GHOST - 1)

    @pl.when(jnp.logical_not(has_high))
    def _():
        no_layer(high_at)

    buffers = (ping, pong)
    for sweep in range(1, SWEEPS):
        old, new = buffers[(sweep - 1) % 2], buffers[sweep % 2]
        final = sweep == SWEEPS - 1
        reach = SWEEPS - 1 - sweep
        wide = main if final else tiles

        def layer(e, _, old=old, new=new, final=final, wide=wide):
            c = [coef(e, k, 1) for k in range(wide)]
            near = [[coef(e, k, n) for n in range(3, COEFS)] for k in range(wide)]
            partial = [[] for _ in range(wide)]
            for t in range(steps):
                here = [old[spot(e, k, t), :] for k in range(tiles)]
                down = [pltpu.roll(value, 1, 0) for value in here]
                up = [pltpu.roll(value, TILE - 1, 0) for value in here]
                for k in range(wide):
                    z_low, x_low, y_low, z_high, x_high, y_high = near[k]
                    below = jnp.where(row == 0, down[k - 1], down[k])
                    above = jnp.where(row == TILE - 1, up[(k + 1) % tiles], up[k])
                    total = source[spot(e, k, t), :] + z_low * old[spot(e - 1, k, t), :]
                    total = total + z_high * old[spot(e + 1, k, t), :]
                    total = total + (x_low * below + x_high * above)
                    total = total + (
                        y_low * pltpu.roll(here[k], 1, 1) + y_high * pltpu.roll(here[k], ny - 1, 1)
                    )
                    if t:
                        total = total + c[k] * partial[k][-1]
                    partial[k].append(total)
            for k in range(wide):
                carry = c[k] * (coef(e, k, 2) * partial[k][-1])
                for t in range(steps):
                    value = partial[k][t] + carry
                    carry = c[k] * carry
                    if final:
                        last[rows_at((t * plan.nz + e - GHOST) * main + k), :] = value
                    else:
                        new[spot(e, k, t), :] = value
            return 0

        start = jnp.where(has_low, GHOST - reach, GHOST)
        stop = jnp.where(has_high, high_at + reach, high_at)
        lax.fori_loop(start, stop, layer, 0)

    size = plan.nz * plan.rows
    for out, (a, m, c) in zip(outs, plan.rounds):
        step = plan.time_of(hi, zb, s, a, m, c)
        out[...] = last[pl.ds(pl.multiple_of(step * size, TILE), size), :]


def place_blocks(plan, place, *refs):
    blocks, out, sems = refs[: plan.steps], refs[plan.steps], refs[plan.steps + 1]
    hi, lo = place[0], place[1]
    copies = []
    for n, (block, (a, m, c)) in enumerate(zip(blocks, plan.rounds)):
        part = (lo % 2) ^ c
        z = pl.multiple_of(((lo // 2) ^ m) * plan.nz, plan.nz)
        x = pl.multiple_of((hi ^ a) * plan.rows, plan.rows)
        target = out.at[part, pl.ds(z, plan.nz), pl.ds(x, plan.rows), :]
        copies.append(pltpu.make_async_copy(block, target, sems.at[n]))
    for copy in copies:
        copy.start()
    for copy in copies:
        copy.wait()


def local(right_side, diffusivity, velocity):
    steps, cores = lax.axis_size("tm"), lax.axis_size("space")
    _, parts, half_z, nx, ny = right_side.shape
    plan = Plan(steps, cores, half_z, nx, ny)
    t, s = lax.axis_index("tm"), lax.axis_index("space")
    hi, lo = t // plan.z_parts, t % plan.z_parts
    place = jnp.stack([hi, lo, s]).astype(jnp.int32)
    size = plan.nz * plan.rows

    blocks = []
    for a, m, c in plan.rounds:
        at = ((lo % 2) ^ c, ((lo // 2) ^ m) * plan.nz, (hi ^ a) * plan.rows, 0)
        block = lax.dynamic_slice(right_side[0], at, (1, plan.nz, plan.rows, ny))
        blocks.append(lax.ppermute(block.reshape(size, ny), FLAT, plan.pairs(a, m, c)))

    packed = kernel_call(
        functools.partial(pack_coefs, plan),
        (4 * half_z * plan.tiles * TILE, ny),
        (place, diffusivity.reshape(half_z * nx, ny), velocity.reshape(3 * half_z * nx, ny)),
    )
    other = lax.ppermute(packed, "space", [(i, cores - 1 - i) for i in range(cores)])
    coefs = kernel_call(
        functools.partial(make_coefs, plan),
        (plan.ext * plan.tiles * COEFS * TILE, ny),
        (place, packed, other),
    )

    sides = 1 if plan.z_parts == 2 else 2
    edge_x = (GHOST * steps * plan.nz, ny)
    edge_z = (GHOST * steps * plan.rows, ny)
    field, x_even, x_odd, *z_sends = kernel_call(
        functools.partial(gather_steps, plan),
        [(steps * size, ny), edge_x, edge_x] + [edge_z] * sides,
        (place, *blocks),
    )
    even = lax.ppermute(x_even, FLAT, plan.x_pairs(0))
    odd = lax.ppermute(x_odd, FLAT, plan.x_pairs(1))
    z_in = [lax.ppermute(send, FLAT, plan.z_pairs(first)) for first, send in enumerate(z_sends)]
    corner = ((GHOST - 1) * steps * TILE, ny)
    planes, *corners = kernel_call(
        functools.partial(gather_ghosts, plan),
        [(TILE * steps * plan.nz, ny)] + [corner] * sides,
        (place, even, odd),
    )
    c_in = [lax.ppermute(send, FLAT, plan.z_pairs(first)) for first, send in enumerate(corners)]

    grid = (plan.ext * plan.tiles * steps * TILE, ny)
    solved = kernel_call(
        functools.partial(sweep_kernel, plan),
        [(size, ny)] * steps,
        (place, coefs, field, planes, *z_in, *c_in),
        scratch=[pltpu.VMEM(grid, jnp.float32)] * 3 + [pltpu.VMEM((steps * size, ny), jnp.float32)],
    )
    back = []
    for block, (a, m, c) in zip(solved, plan.rounds):
        pairs = [(target, source) for source, target in plan.pairs(a, m, c)]
        back.append(lax.ppermute(block, FLAT, pairs).reshape(plan.nz, plan.rows, ny))

    out = pl.pallas_call(
        functools.partial(place_blocks, plan),
        out_shape=jax.ShapeDtypeStruct((parts, half_z, nx, ny), jnp.float32),
        in_specs=[pl.BlockSpec(memory_space=pltpu.SMEM)] + [pl.BlockSpec(memory_space=pl.ANY)] * steps,
        out_specs=pl.BlockSpec(memory_space=pl.ANY),
        scratch_shapes=[pltpu.SemaphoreType.DMA((steps,))],
    )(place, *back)
    return out[None]


def solution(mesh):
    placed = (
        P(("group", "tm"), None, "space", None, None),
        P("space", None, None),
        P(None, "space", None, None),
    )
    return jax.shard_map(
        local,
        mesh=mesh,
        in_specs=placed,
        out_specs=P(("group", "tm"), None, "space", None, None),
        check_vma=False,
    )
```

```python
import functools

import jax
import jax.numpy as jnp
from jax import lax
from jax.experimental import pallas as pl
from jax.experimental.pallas import tpu as pltpu
from jax.sharding import PartitionSpec as P

SWEEPS = 4
GHOST = SWEEPS - 1
QUARTERS = 4
TILE = 8
COEFS = 9

alpha_circ = 0.1
inv_step = 2.0

FLAT = ("tm", "space")


class Plan:
    def __init__(self, steps, cores, half_z, nx, ny):
        self.steps, self.cores, self.half_z, self.nx, self.ny = steps, cores, half_z, nx, ny
        self.z_parts = steps // QUARTERS
        self.in_half = self.z_parts // cores
        self.nz = half_z // self.in_half
        self.rows = nx // QUARTERS
        self.main = self.rows // TILE
        self.tiles = self.main + 1
        self.ext = self.nz + 2 * GHOST
        kinds = [(2, 0), (1, 0), (1, 1), (0, 0), (2, 1), (3, 0), (3, 1), (0, 1)]
        self.rounds = [(a, m, c) for m in range(self.in_half) for a, c in kinds]

    def flat(self, hi, zb, s):
        return (hi * self.z_parts + zb) * self.cores + s

    def pairs(self, a, m, c):
        result = []
        for hi in range(QUARTERS):
            for jm in range(self.in_half):
                for jb in range(2):
                    for h in range(self.cores):
                        source = self.flat(hi, jm * 2 + jb, h)
                        target = self.flat(hi ^ a, h * self.in_half + (jm ^ m), jb ^ c)
                        result.append((source, target))
        return result

    def x_pairs(self, first):
        result = []
        for hi in range(first, QUARTERS - 1, 2):
            for zb in range(self.z_parts):
                for s in range(self.cores):
                    one, two = self.flat(hi, zb, s), self.flat(hi + 1, zb, s)
                    result += [(one, two), (two, one)]
        return result

    def z_pairs(self, first):
        result = []
        for zb in range(first, self.z_parts - 1, 2):
            for hi in range(QUARTERS):
                for s in range(self.cores):
                    one, two = self.flat(hi, zb, s), self.flat(hi, zb + 1, s)
                    result += [(one, two), (two, one)]
        return result

    def time_of(self, hi, zb, s, a, m, c):
        return ((hi ^ a) * self.in_half + ((zb % self.in_half) ^ m)) * 2 + (s ^ c)


def kernel_call(body, outs, args, scratch=(), out_space=pltpu.VMEM, limit=16):
    in_specs = [pl.BlockSpec(memory_space=pltpu.SMEM)]
    in_specs += [pl.BlockSpec(memory_space=pltpu.VMEM)] * (len(args) - 1)
    single = isinstance(outs, tuple)
    shapes = [outs] if single else list(outs)
    result = pl.pallas_call(
        body,
        out_shape=[jax.ShapeDtypeStruct(s, jnp.float32) for s in shapes],
        in_specs=in_specs,
        out_specs=[pl.BlockSpec(memory_space=out_space)] * len(shapes),
        scratch_shapes=list(scratch),
        compiler_params=pltpu.CompilerParams(vmem_limit_bytes=limit << 20),
    )(*args)
    return result[0] if single else result


def rows_at(index, count=1):
    return pl.ds(pl.multiple_of(index * TILE, TILE), count * TILE)


def sublane(plan):
    return lax.broadcasted_iota(jnp.int32, (TILE, plan.ny), 0)


def lane(plan):
    return lax.broadcasted_iota(jnp.int32, (TILE, plan.ny), 1)


def pack_coefs(plan, place, d_ref, v_ref, out_ref):
    hi = place[0]
    per = plan.nx // TILE
    below = jnp.maximum(hi * plan.main - 1, 0)
    above = jnp.minimum(hi * plan.main + plan.main, per - 1)
    row = sublane(plan)

    def layer(z, _):
        for n in range(4):
            ref, base = (d_ref, z * per) if n == 0 else (v_ref, ((n - 1) * plan.half_z + z) * per)
            at = (n * plan.half_z + z) * plan.tiles
            for k in range(plan.main):
                out_ref[rows_at(at + k), :] = ref[rows_at(base + hi * plan.main + k), :]
            over, under = ref[rows_at(base + above), :], ref[rows_at(base + below), :]
            edge = jnp.where(row < TILE // 2, over, under)
            out_ref[rows_at(at + plan.main), :] = edge
        return 0

    lax.fori_loop(0, plan.half_z, layer, 0)


def make_coefs(plan, place, own_ref, other_ref, out_ref):
    hi, zb, s = place[0], place[1], place[2]
    row, col = sublane(plan), lane(plan)

    def layer(e, _):
        depth = zb * plan.nz + e - GHOST
        inside = (depth >= 0) & (depth < plan.half_z * plan.cores)
        depth = jnp.clip(depth, 0, plan.half_z * plan.cores - 1)
        mine = depth // plan.half_z == s
        z = depth % plan.half_z
        for k in range(plan.tiles):
            values = []
            for n in range(4):
                at = rows_at((n * plan.half_z + z) * plan.tiles + k)
                values.append(jnp.where(mine, own_ref[at, :], other_ref[at, :]))
            d, vz, vx, vy = values
            if k < plan.main:
                x = row + k * TILE
            else:
                x = jnp.where(row < GHOST, row + plan.rows, row - TILE)
            x = x + hi * plan.rows
            keep = (x >= 0) & (x < plan.nx) & inside
            if k == plan.main:
                keep = keep & ((row < GHOST) | (row >= TILE - GHOST))
            total = inv_step + 6.0 * d + (jnp.abs(vz) + jnp.abs(vx) + jnp.abs(vy))
            w = jnp.where(keep, 1.0 / total, 0.0)
            c = inv_step * w
            power = c
            for _ in range(plan.steps.bit_length() - 1):
                power = power * power
            wrap = alpha_circ / (1.0 - alpha_circ * power)
            low = [w * (d + jnp.maximum(v, 0.0)) for v in (vz, vx, vy)]
            high = [w * (d + jnp.maximum(-v, 0.0)) for v in (vz, vx, vy)]
            low[2] = jnp.where(col == 0, 0.0, low[2])
            high[2] = jnp.where(col == plan.ny - 1, 0.0, high[2])
            made = [w, c, wrap] + low + high
            for n, value in enumerate(made):
                out_ref[rows_at((e * plan.tiles + k) * COEFS + n), :] = value
        return 0

    lax.fori_loop(0, plan.ext, layer, 0)


def gather_steps(plan, place, *refs):
    hi, zb, s = place[0], place[1], place[2]
    blocks, (field, x_even, x_odd, *z_sends) = refs[: plan.steps], refs[plan.steps :]
    size = plan.nz * plan.rows
    hi_odd = hi % 2 == 1
    zb_odd = zb % 2 == 1
    for block, (a, m, c) in zip(blocks, plan.rounds):
        step = plan.time_of(hi, zb, s, a, m, c)
        field[pl.ds(pl.multiple_of(step * size, TILE), size), :] = block[...]
        for r in range(GHOST):
            low = block[pl.ds(r, plan.nz, stride=plan.rows), :]
            high = block[pl.ds(plan.rows - GHOST + r, plan.nz, stride=plan.rows), :]
            at = pl.ds(r * plan.steps * plan.nz + step * plan.nz, plan.nz)
            x_even[at, :] = jnp.where(hi_odd, low, high)
            x_odd[at, :] = jnp.where(hi_odd, high, low)
        edge = GHOST * plan.rows
        at = pl.ds(pl.multiple_of(step * edge, TILE), edge)
        low, high = block[:edge, :], block[size - edge :, :]
        for first, z_send in enumerate(z_sends):
            z_send[at, :] = jnp.where(zb_odd ^ (first == 1), low, high)


def gather_ghosts(plan, place, even_ref, odd_ref, planes, *corners):
    hi, zb = place[0], place[1]
    hi_odd = hi % 2 == 1
    zb_odd = zb % 2 == 1
    count = plan.steps * plan.nz
    for r in range(GHOST):
        even, odd = even_ref[pl.ds(r * count, count), :], odd_ref[pl.ds(r * count, count), :]
        planes[pl.ds(r * count, count), :] = jnp.where(hi_odd, odd, even)
        planes[pl.ds((TILE - GHOST + r) * count, count), :] = jnp.where(hi_odd, even, odd)
    for r in range(GHOST, TILE - GHOST):
        planes[pl.ds(r * count, count), :] = jnp.zeros((count, plan.ny), jnp.float32)
    deep = GHOST - 1
    for step in range(plan.steps):
        for n in range(deep):
            low = planes[pl.ds(step * plan.nz + n, TILE, stride=count), :]
            high = planes[pl.ds(step * plan.nz + plan.nz - deep + n, TILE, stride=count), :]
            for first, corner in enumerate(corners):
                corner[rows_at(step * deep + n), :] = jnp.where(zb_odd ^ (first == 1), low, high)


def sweep_kernel(plan, place, coefs, field, planes, *refs):
    hi, zb, s = place[0], place[1], place[2]
    sides = 1 if plan.z_parts == 2 else 2
    z_in, refs = refs[:sides], refs[sides:]
    c_in, refs = refs[:sides], refs[sides:]
    outs, (source, ping, pong, last) = refs[: plan.steps], refs[plan.steps :]
    steps, tiles, main, ny = plan.steps, plan.tiles, plan.main, plan.ny
    count = steps * plan.nz
    deep = GHOST - 1
    zb_odd = zb % 2 == 1
    row = sublane(plan)
    has_low, has_high = zb > 0, zb < plan.z_parts - 1

    def spot(e, k, t):
        return rows_at((e * tiles + k) * steps + t)

    def coef(e, k, n):
        return coefs[rows_at((e * tiles + k) * COEFS + n), :]

    def solve(c, wrap, scaled):
        partial = [scaled[0]]
        for value in scaled[1:]:
            partial.append(value + c * partial[-1])
        carry = c * (wrap * partial[-1])
        result = []
        for value in partial:
            result.append(value + carry)
            carry = c * carry
        return result

    def first(e, k, values):
        w, c, wrap = (coef(e, k, n) for n in range(3))
        scaled = [w * value for value in values]
        for t, (value, solved) in enumerate(zip(scaled, solve(c, wrap, scaled))):
            source[spot(e, k, t), :] = value
            ping[spot(e, k, t), :] = solved

    def own_layer(z, _):
        e = z + GHOST
        for k in range(main):
            first(e, k, [field[rows_at((t * plan.nz + z) * main + k), :] for t in range(steps)])
        first(e, main, [planes[pl.ds(t * plan.nz + z, TILE, stride=count), :] for t in range(steps)])
        return 0

    lax.fori_loop(0, plan.nz, own_layer, 0)

    empty = jnp.zeros((TILE, ny), jnp.float32)

    def ghost_layers(at, upper, main_ref, corner_ref):
        for n in range(GHOST):
            e = at + n
            for k in range(main):
                first(e, k, [main_ref[rows_at((t * GHOST + n) * main + k), :] for t in range(steps)])
            c_at = n if upper else n - (GHOST - deep)
            if 0 <= c_at < deep:
                first(e, main, [corner_ref[rows_at(t * deep + c_at), :] for t in range(steps)])
            else:
                for t in range(steps):
                    ping[spot(e, main, t), :] = empty
                    source[spot(e, main, t), :] = empty

    def no_layer(e):
        for k in range(tiles):
            for t in range(steps):
                ping[spot(e, k, t), :] = empty
                pong[spot(e, k, t), :] = empty

    high_at = GHOST + plan.nz
    for odd in (False, True):

        @pl.when(has_low & (zb_odd == odd))
        def _():
            pick = 0 if odd else sides - 1
            ghost_layers(0, False, z_in[pick], c_in[pick])

        @pl.when(has_high & (zb_odd == odd))
        def _():
            pick = sides - 1 if odd else 0
            ghost_layers(high_at, True, z_in[pick], c_in[pick])

    @pl.when(jnp.logical_not(has_low))
    def _():
        no_layer(GHOST - 1)

    @pl.when(jnp.logical_not(has_high))
    def _():
        no_layer(high_at)

    buffers = (ping, pong)
    for sweep in range(1, SWEEPS):
        old, new = buffers[(sweep - 1) % 2], buffers[sweep % 2]
        final = sweep == SWEEPS - 1
        reach = SWEEPS - 1 - sweep
        wide = main if final else tiles

        def layer(e, _, old=old, new=new, final=final, wide=wide):
            c = [coef(e, k, 1) for k in range(wide)]
            near = [[coef(e, k, n) for n in range(3, COEFS)] for k in range(wide)]
            partial = [[] for _ in range(wide)]
            for t in range(steps):
                here = [old[spot(e, k, t), :] for k in range(tiles)]
                down = [pltpu.roll(value, 1, 0) for value in here]
                up = [pltpu.roll(value, TILE - 1, 0) for value in here]
                for k in range(wide):
                    z_low, x_low, y_low, z_high, x_high, y_high = near[k]
                    below = jnp.where(row == 0, down[k - 1], down[k])
                    above = jnp.where(row == TILE - 1, up[(k + 1) % tiles], up[k])
                    total = source[spot(e, k, t), :] + z_low * old[spot(e - 1, k, t), :]
                    total = total + z_high * old[spot(e + 1, k, t), :]
                    total = total + (x_low * below + x_high * above)
                    total = total + (
                        y_low * pltpu.roll(here[k], 1, 1) + y_high * pltpu.roll(here[k], ny - 1, 1)
                    )
                    if t:
                        total = total + c[k] * partial[k][-1]
                    partial[k].append(total)
            for k in range(wide):
                carry = c[k] * (coef(e, k, 2) * partial[k][-1])
                for t in range(steps):
                    value = partial[k][t] + carry
                    carry = c[k] * carry
                    if final:
                        last[rows_at((t * plan.nz + e - GHOST) * main + k), :] = value
                    else:
                        new[spot(e, k, t), :] = value
            return 0

        start = jnp.where(has_low, GHOST - reach, GHOST)
        stop = jnp.where(has_high, high_at + reach, high_at)
        lax.fori_loop(start, stop, layer, 0)

    size = plan.nz * plan.rows
    for out, (a, m, c) in zip(outs, plan.rounds):
        step = plan.time_of(hi, zb, s, a, m, c)
        out[...] = last[pl.ds(pl.multiple_of(step * size, TILE), size), :]


def run_sweeps(plan, place, arrays):
    size = plan.nz * plan.rows
    grid = (plan.ext * plan.tiles * plan.steps * TILE, plan.ny)
    return kernel_call(
        functools.partial(sweep_kernel, plan),
        [(size, plan.ny)] * plan.steps,
        (place, *arrays),
        scratch=[pltpu.VMEM(grid, jnp.float32)] * 3 + [pltpu.VMEM((plan.steps * size, plan.ny), jnp.float32)],
        limit=24,
    )


def place_blocks(plan, place, *refs):
    blocks, out, sems = refs[: plan.steps], refs[plan.steps], refs[plan.steps + 1]
    hi, lo = place[0], place[1]
    copies = []
    for n, (block, (a, m, c)) in enumerate(zip(blocks, plan.rounds)):
        part = (lo % 2) ^ c
        z = pl.multiple_of(((lo // 2) ^ m) * plan.nz, plan.nz)
        x = pl.multiple_of((hi ^ a) * plan.rows, plan.rows)
        target = out.at[part, pl.ds(z, plan.nz), pl.ds(x, plan.rows), :]
        copies.append(pltpu.make_async_copy(block, target, sems.at[n]))
    for copy in copies:
        copy.start()
    for copy in copies:
        copy.wait()


def local(right_side, diffusivity, velocity):
    steps, cores = lax.axis_size("tm"), lax.axis_size("space")
    _, parts, half_z, nx, ny = right_side.shape
    plan = Plan(steps, cores, half_z, nx, ny)
    t, s = lax.axis_index("tm"), lax.axis_index("space")
    hi, lo = t // plan.z_parts, t % plan.z_parts
    place = jnp.stack([hi, lo, s]).astype(jnp.int32)
    size = plan.nz * plan.rows

    blocks = []
    for a, m, c in plan.rounds:
        at = ((lo % 2) ^ c, ((lo // 2) ^ m) * plan.nz, (hi ^ a) * plan.rows, 0)
        block = lax.dynamic_slice(right_side[0], at, (1, plan.nz, plan.rows, ny))
        blocks.append(lax.ppermute(block.reshape(size, ny), FLAT, plan.pairs(a, m, c)))

    sides = 1 if plan.z_parts == 2 else 2
    edge_x = (GHOST * steps * plan.nz, ny)
    edge_z = (GHOST * steps * plan.rows, ny)
    field, x_even, x_odd, *z_sends = kernel_call(
        functools.partial(gather_steps, plan),
        [(steps * size, ny), edge_x, edge_x] + [edge_z] * sides,
        (place, *blocks),
    )
    z_in = [lax.ppermute(send, FLAT, plan.z_pairs(first)) for first, send in enumerate(z_sends)]
    even = lax.ppermute(x_even, FLAT, plan.x_pairs(0))
    odd = lax.ppermute(x_odd, FLAT, plan.x_pairs(1))
    after, field = lax.optimization_barrier((diffusivity, field))
    packed = kernel_call(
        functools.partial(pack_coefs, plan),
        (4 * half_z * plan.tiles * TILE, ny),
        (place, after.reshape(half_z * nx, ny), velocity.reshape(3 * half_z * nx, ny)),
    )
    other = lax.ppermute(packed, "space", [(i, cores - 1 - i) for i in range(cores)])
    coefs = kernel_call(
        functools.partial(make_coefs, plan),
        (plan.ext * plan.tiles * COEFS * TILE, ny),
        (place, packed, other),
    )

    corner = ((GHOST - 1) * steps * TILE, ny)
    planes, *corners = kernel_call(
        functools.partial(gather_ghosts, plan),
        [(TILE * steps * plan.nz, ny)] + [corner] * sides,
        (place, even, odd),
    )
    c_in = [lax.ppermute(send, FLAT, plan.z_pairs(first)) for first, send in enumerate(corners)]

    solved = run_sweeps(plan, place, [coefs, field, planes, *z_in, *c_in])
    back = []
    for block, (a, m, c) in zip(solved, plan.rounds):
        pairs = [(target, source) for source, target in plan.pairs(a, m, c)]
        back.append(lax.ppermute(block, FLAT, pairs).reshape(plan.nz, plan.rows, ny))

    out = kernel_call(
        functools.partial(place_blocks, plan),
        (parts, half_z, nx, ny),
        (place, *back),
        scratch=[pltpu.SemaphoreType.DMA((steps,))],
        out_space=pl.ANY,
    )
    return out[None]


def solution(mesh):
    placed = (
        P(("group", "tm"), None, "space", None, None),
        P("space", None, None),
        P(None, "space", None, None),
    )
    return jax.shard_map(
        local,
        mesh=mesh,
        in_specs=placed,
        out_specs=P(("group", "tm"), None, "space", None, None),
        check_vma=False,
    )
```

```python
import functools

import jax
import jax.numpy as jnp
from jax import lax
from jax.experimental import pallas as pl
from jax.experimental.pallas import tpu as pltpu
from jax.sharding import PartitionSpec as P

SWEEPS = 4
GHOST = SWEEPS - 1
QUARTERS = 4
TILE = 8
COEFS = 9
RAW = 4

alpha_circ = 0.1
inv_step = 2.0

FLAT = ("tm", "space")


class Plan:
    def __init__(self, steps, cores, half_z, nx, ny):
        self.steps, self.cores, self.half_z, self.nx, self.ny = steps, cores, half_z, nx, ny
        self.per_quarter = steps // QUARTERS
        self.in_half = self.per_quarter // 2
        self.z_parts = self.in_half * cores
        self.nz = half_z // self.in_half
        self.rows = nx // QUARTERS
        self.main = self.rows // TILE
        self.tiles = self.main + 1
        self.ext = self.nz + 2 * GHOST
        self.sides = 1 if self.z_parts == 2 else 2
        self.z_tiles = GHOST * self.main + GHOST - 1
        self.raw_tiles = GHOST * self.tiles * RAW
        kinds = [(2, 0), (1, 0), (1, 1), (0, 1), (2, 1), (3, 0), (3, 1), (0, 0)]
        self.rounds = [a * self.per_quarter + m * 2 + c for m in range(self.in_half) for a, c in kinds]

    def direct(self, r):
        return r // self.per_quarter < 2

    def pairs(self, r):
        return [(i, i ^ r) for i in range(self.steps)]

    def x_pairs(self, first):
        result = []
        for hi in range(first, QUARTERS - 1, 2):
            for lo in range(self.per_quarter):
                one = hi * self.per_quarter + lo
                result += [(one, one + self.per_quarter), (one + self.per_quarter, one)]
        return result

    def z_pairs(self, first):
        def flat(hi, zb, part):
            return (hi * self.per_quarter + zb % self.in_half * 2 + part) * self.cores + zb // self.in_half

        result = []
        for zb in range(first, self.z_parts - 1, 2):
            for hi in range(QUARTERS):
                for part in range(2):
                    one, two = flat(hi, zb, part), flat(hi, zb + 1, part)
                    result += [(one, two), (two, one)]
        return result


class Place:
    def __init__(self, plan, ref):
        self.t, self.s = ref[0], ref[1]
        self.hi, self.lo = self.t // plan.per_quarter, self.t % plan.per_quarter
        self.zm, self.part = self.lo // 2, self.lo % 2
        self.zb = self.s * plan.in_half + self.zm
        self.hi_odd, self.zb_odd = self.hi % 2 == 1, self.zb % 2 == 1


def kernel_call(body, outs, args, scratch=(), out_space=pltpu.VMEM, limit=16, aliases=None):
    in_specs = [pl.BlockSpec(memory_space=pltpu.SMEM)]
    in_specs += [pl.BlockSpec(memory_space=pltpu.VMEM)] * (len(args) - 1)
    single = isinstance(outs, tuple)
    shapes = [outs] if single else list(outs)
    result = pl.pallas_call(
        body,
        out_shape=[jax.ShapeDtypeStruct(s, jnp.float32) for s in shapes],
        in_specs=in_specs,
        out_specs=[pl.BlockSpec(memory_space=out_space)] * len(shapes),
        scratch_shapes=list(scratch),
        input_output_aliases=aliases or {},
        compiler_params=pltpu.CompilerParams(vmem_limit_bytes=limit << 20),
    )(*args)
    return result[0] if single else result


def rows_at(index, count=1):
    return pl.ds(pl.multiple_of(index * TILE, TILE), count * TILE)


def sublane(plan):
    return lax.broadcasted_iota(jnp.int32, (TILE, plan.ny), 0)


def lane(plan):
    return lax.broadcasted_iota(jnp.int32, (TILE, plan.ny), 1)


def near_tiles(plan, hi):
    per = plan.nx // TILE
    own = [hi * plan.main + k for k in range(plan.main)]
    return own, jnp.minimum(own[-1] + 1, per - 1), jnp.maximum(own[0] - 1, 0)


def write_coefs(plan, hi, inside, k, values, store):
    row, col = sublane(plan), lane(plan)
    d, vz, vx, vy = values
    if k < plan.main:
        x = row + k * TILE
    else:
        x = jnp.where(row < GHOST, row + plan.rows, row - TILE)
    x = x + hi * plan.rows
    keep = (x >= 0) & (x < plan.nx)
    if k == plan.main:
        keep = keep & ((row < GHOST) | (row >= TILE - GHOST))
    if inside is not None:
        keep = keep & inside
    total = inv_step + 6.0 * d + (jnp.abs(vz) + jnp.abs(vx) + jnp.abs(vy))
    w = jnp.where(keep, 1.0 / total, 0.0)
    c = inv_step * w
    power = c
    for _ in range(plan.steps.bit_length() - 1):
        power = power * power
    wrap = alpha_circ / (1.0 - alpha_circ * power)
    low = [w * (d + jnp.maximum(v, 0.0)) for v in (vz, vx, vy)]
    high = [w * (d + jnp.maximum(-v, 0.0)) for v in (vz, vx, vy)]
    low[2] = jnp.where(col == 0, 0.0, low[2])
    high[2] = jnp.where(col == plan.ny - 1, 0.0, high[2])
    for n, value in enumerate([w, c, wrap] + low + high):
        store(n, value)


def make_coefs(plan, place_ref, d_ref, v_ref, out_ref, *raw_refs):
    place = Place(plan, place_ref)
    per = plan.nx // TILE
    row = sublane(plan)
    own, over, under = near_tiles(plan, place.hi)

    def read(z):
        z = place.zm * plan.nz + z
        found = []
        for n in range(RAW):
            ref, base = (d_ref, z * per) if n == 0 else (v_ref, ((n - 1) * plan.half_z + z) * per)
            edge = jnp.where(row < TILE // 2, ref[rows_at(base + over), :], ref[rows_at(base + under), :])
            found.append([ref[rows_at(base + at), :] for at in own] + [edge])
        return [[tiles[k] for tiles in found] for k in range(plan.tiles)]

    def layer(z, _):
        for k, values in enumerate(read(z)):

            def store(n, value, k=k):
                out_ref[rows_at(((z + GHOST) * plan.tiles + k) * COEFS + n), :] = value

            write_coefs(plan, place.hi, None, k, values, store)
        return 0

    lax.fori_loop(0, plan.nz, layer, 0)
    for side, raw in enumerate(raw_refs):
        up = jnp.logical_not(place.zb_odd) if side == 0 else place.zb_odd
        for n in range(GHOST):
            for k, values in enumerate(read(jnp.where(up, plan.nz - GHOST + n, n))):
                for at, value in enumerate(values):
                    raw[rows_at((n * plan.tiles + k) * RAW + at), :] = value


def pack_blocks(plan, place_ref, right, *outs):
    place = Place(plan, place_ref)
    per = plan.nx // TILE
    row = sublane(plan)
    for out, r in zip(outs, plan.rounds):
        target = place.t ^ r
        quarter, lo = target // plan.per_quarter, target % plan.per_quarter
        first = lo % 2 * plan.half_z + lo // 2 * plan.nz
        own, over, under = near_tiles(plan, quarter)
        for z in range(plan.nz):
            base = (first + z) * per
            for k, at in enumerate(own):
                out[rows_at(z * plan.main + k), :] = right[rows_at(base + at), :]
            if plan.direct(r):
                edge = jnp.where(row < TILE // 2, right[rows_at(base + over), :], right[rows_at(base + under), :])
                out[rows_at(plan.nz * plan.main + z), :] = edge


def edge_rows(plan, place_ref, *refs):
    place = Place(plan, place_ref)
    blocks, (x_even, x_odd) = refs[: plan.steps], refs[plan.steps :]
    half = plan.steps // 2
    for block, r in zip(blocks, plan.rounds):
        step = (place.t ^ r) % half
        for n in range(GHOST):
            low = block[pl.ds(n, plan.nz, stride=plan.rows), :]
            high = block[pl.ds(plan.rows - GHOST + n, plan.nz, stride=plan.rows), :]
            at = pl.ds((n * half + step) * plan.nz, plan.nz)
            if plan.direct(r):
                x_odd[at, :] = jnp.where(place.hi_odd, high, low)
            else:
                x_even[at, :] = jnp.where(place.hi_odd, low, high)


def gather_steps(plan, place_ref, *refs):
    place = Place(plan, place_ref)
    blocks, field = refs[: plan.steps], refs[plan.steps]
    size = plan.nz * plan.rows
    for block, r in zip(blocks, plan.rounds):
        at = pl.multiple_of((place.t ^ r) * size, TILE)
        field[pl.ds(at, size), :] = block[pl.ds(0, size), :]


def gather_ghosts(plan, place_ref, field, even_ref, odd_ref, *refs):
    place = Place(plan, place_ref)
    direct = [r for r in plan.rounds if plan.direct(r)]
    blocks, refs = refs[: len(direct)], refs[len(direct) :]
    raws, refs = refs[: plan.sides], refs[plan.sides :]
    ghost, z_sends, planes = refs[0], refs[1:-1], refs[-1]
    half = plan.steps // 2
    count = half * plan.nz
    size = plan.nz * plan.rows
    for block, r in zip(blocks, direct):
        at = pl.multiple_of((place.t ^ r) * plan.nz * TILE, TILE)
        ghost[pl.ds(at, plan.nz * TILE), :] = block[pl.ds(size, plan.nz * TILE), :]
    for n in range(GHOST):
        even, odd = even_ref[pl.ds(n * count, count), :], odd_ref[pl.ds(n * count, count), :]
        planes[pl.ds(n * count, count), :] = jnp.where(place.hi_odd, odd, even)
        planes[pl.ds((TILE - GHOST + n) * count, count), :] = jnp.where(place.hi_odd, even, odd)
    for n in range(GHOST, TILE - GHOST):
        planes[pl.ds(n * count, count), :] = jnp.zeros((count, plan.ny), jnp.float32)
    first = (1 - place.hi // 2) * count
    for n in range(count):
        ghost[rows_at(first + n), :] = planes[pl.ds(n, TILE, stride=count), :]
    deep, tiles = GHOST - 1, plan.z_tiles
    for side, (raw, z_send) in enumerate(zip(raws, z_sends)):
        up = jnp.logical_not(place.zb_odd) if side == 0 else place.zb_odd
        for t in range(plan.steps):
            for n in range(GHOST):
                z = t * plan.nz + jnp.where(up, plan.nz - GHOST + n, n)
                for k in range(plan.main):
                    z_send[rows_at(t * tiles + n * plan.main + k), :] = field[rows_at(z * plan.main + k), :]
            for n in range(deep):
                z = t * plan.nz + jnp.where(up, plan.nz - deep + n, n)
                z_send[rows_at(t * tiles + GHOST * plan.main + n), :] = ghost[rows_at(z), :]
        z_send[rows_at(plan.steps * tiles, plan.raw_tiles), :] = raw[...]


class Sweeps:
    def __init__(self, plan, place, coefs, source, ping, pong, last):
        self.plan, self.coefs = plan, coefs
        self.source, self.buffers, self.last = source, (ping, pong), last
        self.has_low, self.has_high = place.zb > 0, place.zb < plan.z_parts - 1
        self.low_at, self.high_at = GHOST, GHOST + plan.nz

    def spot(self, e, k, t):
        return rows_at((e * self.plan.tiles + k) * self.plan.steps + t)

    def coef(self, e, k, n):
        return self.coefs[rows_at((e * self.plan.tiles + k) * COEFS + n), :]

    def first(self, e, k, values):
        w, c, wrap = (self.coef(e, k, n) for n in range(3))
        partial = []
        for t, value in enumerate(values):
            value = w * value
            self.source[self.spot(e, k, t), :] = value
            if t:
                value = value + c * partial[-1]
            partial.append(value)
        carry = c * (wrap * partial[-1])
        for t, value in enumerate(partial):
            self.buffers[0][self.spot(e, k, t), :] = value + carry
            carry = c * carry

    def sweep(self, number, start, stop):
        plan, steps, tiles, ny = self.plan, self.plan.steps, self.plan.tiles, self.plan.ny
        old, new = self.buffers[(number - 1) % 2], self.buffers[number % 2]
        final = number == SWEEPS - 1
        wide = plan.main if final else tiles
        row = sublane(plan)
        spot, coef = self.spot, self.coef

        def layer(e, _):
            c = [coef(e, k, 1) for k in range(wide)]
            near = [[coef(e, k, n) for n in range(3, COEFS)] for k in range(wide)]
            partial = [[] for _ in range(wide)]
            for t in range(steps):
                here = [old[spot(e, k, t), :] for k in range(tiles)]
                down = [pltpu.roll(value, 1, 0) for value in here]
                up = [pltpu.roll(value, TILE - 1, 0) for value in here]
                for k in range(wide):
                    z_low, x_low, y_low, z_high, x_high, y_high = near[k]
                    below = jnp.where(row == 0, down[k - 1], down[k])
                    above = jnp.where(row == TILE - 1, up[(k + 1) % tiles], up[k])
                    total = self.source[spot(e, k, t), :] + z_low * old[spot(e - 1, k, t), :]
                    total = total + z_high * old[spot(e + 1, k, t), :]
                    total = total + (x_low * below + x_high * above)
                    total = total + (
                        y_low * pltpu.roll(here[k], 1, 1) + y_high * pltpu.roll(here[k], ny - 1, 1)
                    )
                    if t:
                        total = total + c[k] * partial[k][-1]
                    partial[k].append(total)
            for k in range(wide):
                carry = c[k] * (coef(e, k, 2) * partial[k][-1])
                for t in range(steps):
                    value = partial[k][t] + carry
                    carry = c[k] * carry
                    if final:
                        self.last[rows_at((t * plan.nz + e - GHOST) * plan.main + k), :] = value
                    else:
                        new[spot(e, k, t), :] = value
            return 0

        lax.fori_loop(start, stop, layer, 0)


def all_sweeps(plan, place_ref, coefs_in, field, ghost, *refs):
    place = Place(plan, place_ref)
    sides, steps, main = plan.sides, plan.steps, plan.main
    z_in, refs = refs[:sides], refs[sides:]
    outs, (coefs, source, ping, pong, last) = refs[:steps], refs[steps:]
    work = Sweeps(plan, place, coefs, source, ping, pong, last)
    deep = GHOST - 1
    empty = jnp.zeros((TILE, plan.ny), jnp.float32)

    def own_layer(z, _):
        for k in range(main):
            work.first(z + GHOST, k, [field[rows_at((t * plan.nz + z) * main + k), :] for t in range(steps)])
        work.first(z + GHOST, main, [ghost[rows_at(t * plan.nz + z), :] for t in range(steps)])
        return 0

    lax.fori_loop(0, plan.nz, own_layer, 0)

    def ghost_layers(at, upper, z_ref):
        for n in range(GHOST):
            e = at + n
            for k in range(plan.tiles):
                raw = steps * plan.z_tiles + (n * plan.tiles + k) * RAW

                def store(number, value, k=k, e=e):
                    coefs[rows_at((e * plan.tiles + k) * COEFS + number), :] = value

                write_coefs(plan, place.hi, None, k, [z_ref[rows_at(raw + m), :] for m in range(RAW)], store)
            for k in range(main):
                tile = n * main + k
                work.first(e, k, [z_ref[rows_at(t * plan.z_tiles + tile), :] for t in range(steps)])
            c_at = n if upper else n - (GHOST - deep)
            if 0 <= c_at < deep:
                tile = GHOST * main + c_at
                work.first(e, main, [z_ref[rows_at(t * plan.z_tiles + tile), :] for t in range(steps)])
            else:
                for t in range(steps):
                    ping[work.spot(e, main, t), :] = empty
                    source[work.spot(e, main, t), :] = empty

    for odd in (False, True):

        @pl.when(work.has_low & (place.zb_odd == odd))
        def _(odd=odd):
            ghost_layers(0, False, z_in[0 if odd else sides - 1])

        @pl.when(work.has_high & (place.zb_odd == odd))
        def _(odd=odd):
            ghost_layers(work.high_at, True, z_in[sides - 1 if odd else 0])

    for outside, e in ((work.has_low, work.low_at - 1), (work.has_high, work.high_at)):

        @pl.when(jnp.logical_not(outside))
        def _(e=e):
            for k in range(plan.tiles):
                for t in range(steps):
                    for buffer in work.buffers:
                        buffer[work.spot(e, k, t), :] = empty

    for number in range(1, SWEEPS):
        reach = SWEEPS - 1 - number
        start = work.low_at - jnp.where(work.has_low, reach, 0)
        stop = work.high_at + jnp.where(work.has_high, reach, 0)
        work.sweep(number, start, stop)

    size = plan.nz * plan.rows
    for out, r in zip(outs, plan.rounds):
        out[...] = last[pl.ds(pl.multiple_of((place.t ^ r) * size, TILE), size), :]


def run_sweeps(plan, place, coefs, field, ghost, z_in):
    size = plan.nz * plan.rows
    grid = pltpu.VMEM((plan.ext * plan.tiles * plan.steps * TILE, plan.ny), jnp.float32)
    outs = kernel_call(
        functools.partial(all_sweeps, plan),
        [(size, plan.ny)] * plan.steps + [coefs.shape],
        (place, coefs, field, ghost, *z_in),
        scratch=[grid] * 3 + [pltpu.VMEM((plan.steps * size, plan.ny), jnp.float32)],
        aliases={1: plan.steps},
        limit=24,
    )
    return outs[: plan.steps]


def place_blocks(plan, place_ref, *refs):
    place = Place(plan, place_ref)
    blocks, out, sems = refs[: plan.steps], refs[plan.steps], refs[plan.steps + 1]
    copies = []
    for n, (block, r) in enumerate(zip(blocks, plan.rounds)):
        source = place.t ^ r
        quarter, lo = source // plan.per_quarter, source % plan.per_quarter
        z = pl.multiple_of(lo // 2 * plan.nz, plan.nz)
        x = pl.multiple_of(quarter * plan.rows, plan.rows)
        target = out.at[lo % 2, pl.ds(z, plan.nz), pl.ds(x, plan.rows), :]
        copies.append(pltpu.make_async_copy(block, target, sems.at[n]))
    for copy in copies:
        copy.start()
    for copy in copies:
        copy.wait()


def local(right_side, diffusivity, velocity):
    steps, cores = lax.axis_size("tm"), lax.axis_size("space")
    _, parts, half_z, nx, ny = right_side.shape
    plan = Plan(steps, cores, half_z, nx, ny)
    place = jnp.stack([lax.axis_index("tm"), lax.axis_index("space")]).astype(jnp.int32)
    size = plan.nz * plan.rows
    half_x = steps // 2 * plan.nz

    def call(body, outs, arrays, **options):
        return kernel_call(functools.partial(body, plan), outs, (place, *arrays), **options)

    def turned(arrays):
        return [array if r == 0 else lax.ppermute(array, "tm", plan.pairs(r)) for array, r in zip(arrays, plan.rounds)]

    with_ghosts = (size + plan.nz * TILE, ny)
    blocks = turned(
        call(
            pack_blocks,
            [with_ghosts if plan.direct(r) else (size, ny) for r in plan.rounds],
            (right_side.reshape(parts * half_z * nx, ny),),
        )
    )
    blocks = lax.optimization_barrier(blocks)
    x_even, x_odd = call(edge_rows, [(GHOST * half_x, ny)] * 2, blocks)
    even = lax.ppermute(x_even, "tm", plan.x_pairs(0))
    odd = lax.ppermute(x_odd, "tm", plan.x_pairs(1))
    diffusivity, velocity, *blocks = lax.optimization_barrier((diffusivity, velocity, *blocks))
    field = call(gather_steps, (steps * size, ny), blocks)
    coefs, *raws = call(
        make_coefs,
        [(plan.ext * plan.tiles * COEFS * TILE, ny)] + [(plan.raw_tiles * TILE, ny)] * plan.sides,
        (diffusivity.reshape(half_z * nx, ny), velocity.reshape(3 * half_z * nx, ny)),
    )
    direct = [block for block, r in zip(blocks, plan.rounds) if plan.direct(r)]
    ghost, *z_sends = call(
        gather_ghosts,
        [(steps * plan.nz * TILE, ny)] + [((steps * plan.z_tiles + plan.raw_tiles) * TILE, ny)] * plan.sides,
        (field, even, odd, *direct, *raws),
        scratch=[pltpu.VMEM((half_x * TILE, ny), jnp.float32)],
    )
    z_in = [lax.ppermute(send, FLAT, plan.z_pairs(first)) for first, send in enumerate(z_sends)]
    solved = run_sweeps(plan, place, coefs, field, ghost, z_in)
    back = [block.reshape(plan.nz, plan.rows, ny) for block in turned(solved)]
    out = call(
        place_blocks,
        (parts, half_z, nx, ny),
        back,
        scratch=[pltpu.SemaphoreType.DMA((steps,))],
        out_space=pl.ANY,
    )
    return out[None]


def solution(mesh):
    placed = (
        P(("group", "tm"), None, "space", None, None),
        P("space", None, None),
        P(None, "space", None, None),
    )
    return jax.shard_map(
        local,
        mesh=mesh,
        in_specs=placed,
        out_specs=P(("group", "tm"), None, "space", None, None),
        check_vma=False,
    )
```

```python
import functools

import jax
import jax.numpy as jnp
from jax import lax
from jax.experimental import pallas as pl
from jax.experimental.pallas import tpu as pltpu
from jax.sharding import PartitionSpec as P

SWEEPS = 4
GHOST = SWEEPS - 1
QUARTERS = 4
TILE = 8
COEFS = 9
RAW = 4
GROUP = 6

alpha_circ = 0.1
inv_step = 2.0

FLAT = ("tm", "space")


class Plan:
    def __init__(self, steps, cores, half_z, nx, ny):
        self.steps, self.cores, self.half_z, self.nx, self.ny = steps, cores, half_z, nx, ny
        self.per_quarter = steps // QUARTERS
        self.in_half = self.per_quarter // 2
        self.z_parts = self.in_half * cores
        self.nz = half_z // self.in_half
        self.rows = nx // QUARTERS
        self.main = self.rows // TILE
        self.tiles = self.main + 1
        self.ext = self.nz + 2 * GHOST
        self.sides = 1 if self.z_parts == 2 else 2
        self.z_tiles = GHOST * self.main + GHOST - 1
        self.raw_tiles = GHOST * self.tiles * RAW
        kinds = [(2, 0), (1, 0), (1, 1), (0, 1), (2, 1), (3, 0), (3, 1), (0, 0)]
        self.rounds = [a * self.per_quarter + m * 2 + c for m in range(self.in_half) for a, c in kinds]

    def direct(self, r):
        return r // self.per_quarter < 2

    def stride(self, r):
        return self.rows + TILE if self.direct(r) else self.rows

    def pairs(self, r):
        return [(i, i ^ r) for i in range(self.steps)]

    def x_pairs(self, first):
        result = []
        for hi in range(first, QUARTERS - 1, 2):
            for lo in range(self.per_quarter):
                one = hi * self.per_quarter + lo
                result += [(one, one + self.per_quarter), (one + self.per_quarter, one)]
        return result

    def z_pairs(self, first):
        def flat(hi, zb, part):
            return (hi * self.per_quarter + zb % self.in_half * 2 + part) * self.cores + zb // self.in_half

        result = []
        for zb in range(first, self.z_parts - 1, 2):
            for hi in range(QUARTERS):
                for part in range(2):
                    one, two = flat(hi, zb, part), flat(hi, zb + 1, part)
                    result += [(one, two), (two, one)]
        return result


class Place:
    def __init__(self, plan, ref):
        self.t, self.s = ref[0], ref[1]
        self.hi, self.lo = self.t // plan.per_quarter, self.t % plan.per_quarter
        self.zm, self.part = self.lo // 2, self.lo % 2
        self.zb = self.s * plan.in_half + self.zm
        self.hi_odd, self.zb_odd = self.hi % 2 == 1, self.zb % 2 == 1


def kernel_call(body, outs, args, scratch=(), spaces=None, out_space=pltpu.VMEM, limit=16, aliases=None):
    spaces = [pltpu.SMEM] + (spaces or [pltpu.VMEM] * (len(args) - 1))
    single = isinstance(outs, tuple)
    shapes = [outs] if single else list(outs)
    result = pl.pallas_call(
        body,
        out_shape=[jax.ShapeDtypeStruct(s, jnp.float32) for s in shapes],
        in_specs=[pl.BlockSpec(memory_space=space) for space in spaces],
        out_specs=[pl.BlockSpec(memory_space=out_space)] * len(shapes),
        scratch_shapes=list(scratch),
        input_output_aliases=aliases or {},
        compiler_params=pltpu.CompilerParams(vmem_limit_bytes=limit << 20),
    )(*args)
    return result[0] if single else result


def rows_at(index, count=1):
    return pl.ds(pl.multiple_of(index * TILE, TILE), count * TILE)


def sublane(plan):
    return lax.broadcasted_iota(jnp.int32, (TILE, plan.ny), 0)


def lane(plan):
    return lax.broadcasted_iota(jnp.int32, (TILE, plan.ny), 1)


def near_tiles(plan, hi):
    per = plan.nx // TILE
    own = [hi * plan.main + k for k in range(plan.main)]
    return own, jnp.minimum(own[-1] + 1, per - 1), jnp.maximum(own[0] - 1, 0)


def write_coefs(plan, hi, inside, k, values, store):
    row, col = sublane(plan), lane(plan)
    d, vz, vx, vy = values
    if k < plan.main:
        x = row + k * TILE
    else:
        x = jnp.where(row < GHOST, row + plan.rows, row - TILE)
    x = x + hi * plan.rows
    keep = (x >= 0) & (x < plan.nx)
    if k == plan.main:
        keep = keep & ((row < GHOST) | (row >= TILE - GHOST))
    if inside is not None:
        keep = keep & inside
    total = inv_step + 6.0 * d + (jnp.abs(vz) + jnp.abs(vx) + jnp.abs(vy))
    w = jnp.where(keep, 1.0 / total, 0.0)
    c = inv_step * w
    power = c
    for _ in range(plan.steps.bit_length() - 1):
        power = power * power
    wrap = alpha_circ / (1.0 - alpha_circ * power)
    low = [w * (d + jnp.maximum(v, 0.0)) for v in (vz, vx, vy)]
    high = [w * (d + jnp.maximum(-v, 0.0)) for v in (vz, vx, vy)]
    low[2] = jnp.where(col == 0, 0.0, low[2])
    high[2] = jnp.where(col == plan.ny - 1, 0.0, high[2])
    for n, value in enumerate([w, c, wrap] + low + high):
        store(n, value)


def make_coefs(plan, place_ref, d_ref, v_ref, out_ref, *raw_refs):
    place = Place(plan, place_ref)
    per = plan.nx // TILE
    row = sublane(plan)
    own, over, under = near_tiles(plan, place.hi)

    def read(z):
        z = place.zm * plan.nz + z
        found = []
        for n in range(RAW):
            ref, base = (d_ref, z * per) if n == 0 else (v_ref, ((n - 1) * plan.half_z + z) * per)
            edge = jnp.where(row < TILE // 2, ref[rows_at(base + over), :], ref[rows_at(base + under), :])
            found.append([ref[rows_at(base + at), :] for at in own] + [edge])
        return [[tiles[k] for tiles in found] for k in range(plan.tiles)]

    def layer(z, _):
        for k, values in enumerate(read(z)):

            def store(n, value, k=k):
                out_ref[rows_at(((z + GHOST) * plan.tiles + k) * COEFS + n), :] = value

            write_coefs(plan, place.hi, None, k, values, store)
        return 0

    lax.fori_loop(0, plan.nz, layer, 0)
    for side, raw in enumerate(raw_refs):
        up = jnp.logical_not(place.zb_odd) if side == 0 else place.zb_odd
        for n in range(GHOST):
            for k, values in enumerate(read(jnp.where(up, plan.nz - GHOST + n, n))):
                for at, value in enumerate(values):
                    raw[rows_at((n * plan.tiles + k) * RAW + at), :] = value


def pack_blocks(plan, rounds, place_ref, right, *outs):
    place = Place(plan, place_ref)
    per = plan.nx // TILE
    row = sublane(plan)
    for out, r in zip(outs, rounds):
        target = place.t ^ r
        quarter, lo = target // plan.per_quarter, target % plan.per_quarter
        first = lo % 2 * plan.half_z + lo // 2 * plan.nz
        own, over, under = near_tiles(plan, quarter)
        tiles = plan.stride(r) // TILE
        for z in range(plan.nz):
            base = (first + z) * per
            for k, at in enumerate(own):
                out[rows_at(z * tiles + k), :] = right[rows_at(base + at), :]
            if plan.direct(r):
                edge = jnp.where(row < TILE // 2, right[rows_at(base + over), :], right[rows_at(base + under), :])
                out[rows_at(z * tiles + plan.main), :] = edge


def edge_rows(plan, place_ref, *refs):
    place = Place(plan, place_ref)
    blocks, (x_even, x_odd) = refs[: plan.steps], refs[plan.steps :]
    half = plan.steps // 2
    for block, r in zip(blocks, plan.rounds):
        step = (place.t ^ r) % half
        stride = plan.stride(r)
        for n in range(GHOST):
            low = block[pl.ds(n, plan.nz, stride=stride), :]
            high = block[pl.ds(plan.rows - GHOST + n, plan.nz, stride=stride), :]
            at = pl.ds((n * half + step) * plan.nz, plan.nz)
            if plan.direct(r):
                x_odd[at, :] = jnp.where(place.hi_odd, high, low)
            else:
                x_even[at, :] = jnp.where(place.hi_odd, low, high)


def gather_steps(plan, place_ref, *refs):
    place = Place(plan, place_ref)
    blocks, field = refs[: plan.steps], refs[plan.steps]
    size = plan.nz * plan.rows
    for block, r in zip(blocks, plan.rounds):
        at = (place.t ^ r) * size
        for z in range(plan.nz):
            to = pl.ds(pl.multiple_of(at + z * plan.rows, TILE), plan.rows)
            field[to, :] = block[pl.ds(z * plan.stride(r), plan.rows), :]


def gather_ghosts(plan, place_ref, field, even_ref, odd_ref, *refs):
    place = Place(plan, place_ref)
    direct = [r for r in plan.rounds if plan.direct(r)]
    blocks, refs = refs[: len(direct)], refs[len(direct) :]
    raws, refs = refs[: plan.sides], refs[plan.sides :]
    ghost, z_sends, planes = refs[0], refs[1:-1], refs[-1]
    half = plan.steps // 2
    count = half * plan.nz
    for block, r in zip(blocks, direct):
        at = (place.t ^ r) * plan.nz
        for z in range(plan.nz):
            ghost[rows_at(at + z), :] = block[pl.ds(z * plan.stride(r) + plan.rows, TILE), :]
    for n in range(GHOST):
        even, odd = even_ref[pl.ds(n * count, count), :], odd_ref[pl.ds(n * count, count), :]
        planes[pl.ds(n * count, count), :] = jnp.where(place.hi_odd, odd, even)
        planes[pl.ds((TILE - GHOST + n) * count, count), :] = jnp.where(place.hi_odd, even, odd)
    for n in range(GHOST, TILE - GHOST):
        planes[pl.ds(n * count, count), :] = jnp.zeros((count, plan.ny), jnp.float32)
    first = (1 - place.hi // 2) * count
    for n in range(count):
        ghost[rows_at(first + n), :] = planes[pl.ds(n, TILE, stride=count), :]
    deep, tiles = GHOST - 1, plan.z_tiles
    for side, (raw, z_send) in enumerate(zip(raws, z_sends)):
        up = jnp.logical_not(place.zb_odd) if side == 0 else place.zb_odd
        for t in range(plan.steps):
            for n in range(GHOST):
                z = t * plan.nz + jnp.where(up, plan.nz - GHOST + n, n)
                for k in range(plan.main):
                    z_send[rows_at(t * tiles + n * plan.main + k), :] = field[rows_at(z * plan.main + k), :]
            for n in range(deep):
                z = t * plan.nz + jnp.where(up, plan.nz - deep + n, n)
                z_send[rows_at(t * tiles + GHOST * plan.main + n), :] = ghost[rows_at(z), :]
        z_send[rows_at(plan.steps * tiles, plan.raw_tiles), :] = raw[...]


class Sweeps:
    def __init__(self, plan, place, coefs, source, ping, pong, last):
        self.plan, self.coefs = plan, coefs
        self.source, self.buffers, self.last = source, (ping, pong), last
        self.has_low, self.has_high = place.zb > 0, place.zb < plan.z_parts - 1
        self.low_at, self.high_at = GHOST, GHOST + plan.nz

    def spot(self, e, k, t):
        return rows_at((e * self.plan.tiles + k) * self.plan.steps + t)

    def coef(self, e, k, n):
        return self.coefs[rows_at((e * self.plan.tiles + k) * COEFS + n), :]

    def first(self, e, k, values):
        w, c, wrap = (self.coef(e, k, n) for n in range(3))
        partial = []
        for t, value in enumerate(values):
            value = w * value
            self.source[self.spot(e, k, t), :] = value
            if t:
                value = value + c * partial[-1]
            partial.append(value)
        carry = c * (wrap * partial[-1])
        for t, value in enumerate(partial):
            self.buffers[0][self.spot(e, k, t), :] = value + carry
            carry = c * carry

    def sweep(self, number, start, stop):
        plan, steps, tiles, ny = self.plan, self.plan.steps, self.plan.tiles, self.plan.ny
        old, new = self.buffers[(number - 1) % 2], self.buffers[number % 2]
        final = number == SWEEPS - 1
        wide = plan.main if final else tiles
        row = sublane(plan)
        spot, coef = self.spot, self.coef

        def layers(e, count):
            parts = [(e + g, k) for g in range(count) for k in range(wide)]
            c = [coef(at, k, 1) for at, k in parts]
            near = [[coef(at, k, n) for n in range(3, COEFS)] for at, k in parts]
            partial = [[] for _ in parts]
            for g in range(count):
                at = e + g
                for t in range(steps):
                    here = [old[spot(at, k, t), :] for k in range(tiles)]
                    down = [pltpu.roll(value, 1, 0) for value in here]
                    up = [pltpu.roll(value, TILE - 1, 0) for value in here]
                    for k in range(wide):
                        n = g * wide + k
                        z_low, x_low, y_low, z_high, x_high, y_high = near[n]
                        below = jnp.where(row == 0, down[k - 1], down[k])
                        above = jnp.where(row == TILE - 1, up[(k + 1) % tiles], up[k])
                        total = self.source[spot(at, k, t), :] + z_low * old[spot(at - 1, k, t), :]
                        total = total + z_high * old[spot(at + 1, k, t), :]
                        total = total + (x_low * below + x_high * above)
                        total = total + (
                            y_low * pltpu.roll(here[k], 1, 1) + y_high * pltpu.roll(here[k], ny - 1, 1)
                        )
                        if t:
                            total = total + c[n] * partial[n][-1]
                        partial[n].append(total)
            for n, (at, k) in enumerate(parts):
                carry = c[n] * (coef(at, k, 2) * partial[n][-1])
                for t in range(steps):
                    value = partial[n][t] + carry
                    carry = c[n] * carry
                    if final:
                        self.last[rows_at((t * plan.nz + at - GHOST) * plan.main + k), :] = value
                    else:
                        new[spot(at, k, t), :] = value

        if plan.sides == 1:
            total = plan.nz + SWEEPS - 1 - number

            def several(i, _):
                layers(start + i * GROUP, GROUP)
                return 0

            lax.fori_loop(0, total // GROUP, several, 0)
            if total % GROUP:
                layers(start + total // GROUP * GROUP, total % GROUP)
        else:

            def one(e, _):
                layers(e, 1)
                return 0

            lax.fori_loop(start, stop, one, 0)


def all_sweeps(plan, place_ref, coefs_in, field, ghost, *refs):
    place = Place(plan, place_ref)
    sides, steps, main = plan.sides, plan.steps, plan.main
    z_in, refs = refs[:sides], refs[sides:]
    outs, (coefs, source, ping, pong, last) = refs[:steps], refs[steps:]
    work = Sweeps(plan, place, coefs, source, ping, pong, last)
    deep = GHOST - 1
    empty = jnp.zeros((TILE, plan.ny), jnp.float32)

    def own_layers(i, _):
        for n in range(4):
            z = i * 4 + n
            for k in range(main):
                work.first(z + GHOST, k, [field[rows_at((t * plan.nz + z) * main + k), :] for t in range(steps)])
            work.first(z + GHOST, main, [ghost[rows_at(t * plan.nz + z), :] for t in range(steps)])
        return 0

    lax.fori_loop(0, plan.nz // 4, own_layers, 0)

    def ghost_layers(at, upper, z_ref):
        for n in range(GHOST):
            e = at + n
            for k in range(plan.tiles):
                raw = steps * plan.z_tiles + (n * plan.tiles + k) * RAW

                def store(number, value, k=k, e=e):
                    coefs[rows_at((e * plan.tiles + k) * COEFS + number), :] = value

                write_coefs(plan, place.hi, None, k, [z_ref[rows_at(raw + m), :] for m in range(RAW)], store)
            for k in range(main):
                tile = n * main + k
                work.first(e, k, [z_ref[rows_at(t * plan.z_tiles + tile), :] for t in range(steps)])
            c_at = n if upper else n - (GHOST - deep)
            if 0 <= c_at < deep:
                tile = GHOST * main + c_at
                work.first(e, main, [z_ref[rows_at(t * plan.z_tiles + tile), :] for t in range(steps)])
            else:
                for t in range(steps):
                    ping[work.spot(e, main, t), :] = empty
                    source[work.spot(e, main, t), :] = empty

    for odd in (False, True):

        @pl.when(work.has_low & (place.zb_odd == odd))
        def _(odd=odd):
            ghost_layers(0, False, z_in[0 if odd else sides - 1])

        @pl.when(work.has_high & (place.zb_odd == odd))
        def _(odd=odd):
            ghost_layers(work.high_at, True, z_in[sides - 1 if odd else 0])

    for outside, e in ((work.has_low, work.low_at - 1), (work.has_high, work.high_at)):

        @pl.when(jnp.logical_not(outside))
        def _(e=e):
            for k in range(plan.tiles):
                for t in range(steps):
                    for buffer in work.buffers:
                        buffer[work.spot(e, k, t), :] = empty

    for number in range(1, SWEEPS):
        reach = SWEEPS - 1 - number
        start = work.low_at - jnp.where(work.has_low, reach, 0)
        stop = work.high_at + jnp.where(work.has_high, reach, 0)
        work.sweep(number, start, stop)

    size = plan.nz * plan.rows
    for out, r in zip(outs, plan.rounds):
        out[...] = last[pl.ds(pl.multiple_of((place.t ^ r) * size, TILE), size), :]


def run_sweeps(plan, place, coefs, field, ghost, z_in):
    size = plan.nz * plan.rows
    grid = pltpu.VMEM((plan.ext * plan.tiles * plan.steps * TILE, plan.ny), jnp.float32)
    outs = kernel_call(
        functools.partial(all_sweeps, plan),
        [(size, plan.ny)] * plan.steps + [coefs.shape],
        (place, coefs, field, ghost, *z_in),
        scratch=[grid] * 3 + [pltpu.VMEM((plan.steps * size, plan.ny), jnp.float32)],
        aliases={1: plan.steps},
        limit=24,
    )
    return outs[: plan.steps]


def place_blocks(plan, place_ref, *refs):
    place = Place(plan, place_ref)
    blocks, (out, sems) = refs[: plan.steps], refs[plan.steps :]
    copies = []
    for n, (block, r) in enumerate(zip(blocks, plan.rounds)):
        source = place.t ^ r
        quarter, lo = source // plan.per_quarter, source % plan.per_quarter
        z = pl.multiple_of(lo // 2 * plan.nz, plan.nz)
        x = pl.multiple_of(quarter * plan.rows, plan.rows)
        target = out.at[lo % 2, pl.ds(z, plan.nz), pl.ds(x, plan.rows), :]
        copies.append(pltpu.make_async_copy(block, target, sems.at[n]))
    for copy in copies:
        copy.start()
    for copy in copies:
        copy.wait()


def local(right_side, diffusivity, velocity):
    steps, cores = lax.axis_size("tm"), lax.axis_size("space")
    _, parts, half_z, nx, ny = right_side.shape
    plan = Plan(steps, cores, half_z, nx, ny)
    place = jnp.stack([lax.axis_index("tm"), lax.axis_index("space")]).astype(jnp.int32)
    size = plan.nz * plan.rows
    half_x = steps // 2 * plan.nz

    def call(body, outs, arrays, rounds=None, **options):
        body = functools.partial(body, plan) if rounds is None else functools.partial(body, plan, rounds)
        return kernel_call(body, outs, (place, *arrays), **options)

    def turned(arrays):
        return [array if r == 0 else lax.ppermute(array, "tm", plan.pairs(r)) for array, r in zip(arrays, plan.rounds)]

    sends = call(
        pack_blocks,
        [(plan.nz * plan.stride(r), ny) for r in plan.rounds],
        (right_side.reshape(parts * half_z * nx, ny),),
        rounds=plan.rounds,
    )
    blocks = turned(sends)
    blocks = lax.optimization_barrier(blocks)
    x_even, x_odd = call(edge_rows, [(GHOST * half_x, ny)] * 2, blocks)
    even = lax.ppermute(x_even, "tm", plan.x_pairs(0))
    odd = lax.ppermute(x_odd, "tm", plan.x_pairs(1))
    diffusivity, velocity, *blocks = lax.optimization_barrier((diffusivity, velocity, *blocks))
    field = call(gather_steps, (steps * size, ny), blocks)
    coefs, *raws = call(
        make_coefs,
        [(plan.ext * plan.tiles * COEFS * TILE, ny)] + [(plan.raw_tiles * TILE, ny)] * plan.sides,
        (diffusivity.reshape(half_z * nx, ny), velocity.reshape(3 * half_z * nx, ny)),
    )
    direct = [block for block, r in zip(blocks, plan.rounds) if plan.direct(r)]
    ghost, *z_sends = call(
        gather_ghosts,
        [(steps * plan.nz * TILE, ny)] + [((steps * plan.z_tiles + plan.raw_tiles) * TILE, ny)] * plan.sides,
        (field, even, odd, *direct, *raws),
        scratch=[pltpu.VMEM((half_x * TILE, ny), jnp.float32)],
    )
    z_in = [lax.ppermute(send, FLAT, plan.z_pairs(first)) for first, send in enumerate(z_sends)]
    solved = run_sweeps(plan, place, coefs, field, ghost, z_in)
    back = [block.reshape(plan.nz, plan.rows, ny) for block in turned(solved)]
    out = call(
        place_blocks,
        (parts, half_z, nx, ny),
        back,
        scratch=[pltpu.SemaphoreType.DMA((steps,))],
        out_space=pl.ANY,
    )
    return out[None]


def solution(mesh):
    placed = (
        P(("group", "tm"), None, "space", None, None),
        P("space", None, None),
        P(None, "space", None, None),
    )
    return jax.shard_map(
        local,
        mesh=mesh,
        in_specs=placed,
        out_specs=P(("group", "tm"), None, "space", None, None),
        check_vma=False,
    )
```

```python
import functools

import jax
import jax.numpy as jnp
from jax import lax
from jax.experimental import pallas as pl
from jax.experimental.pallas import tpu as pltpu
from jax.sharding import PartitionSpec as P

SWEEPS = 4
GHOST = SWEEPS - 1
QUARTERS = 4
TILE = 8
COEFS = 9
RAW = 4
GROUP = 6

alpha_circ = 0.1
inv_step = 2.0

FLAT = ("tm", "space")


class Plan:
    def __init__(self, steps, cores, half_z, nx, ny):
        self.steps, self.cores, self.half_z, self.nx, self.ny = steps, cores, half_z, nx, ny
        self.per_quarter = steps // QUARTERS
        self.in_half = self.per_quarter // 2
        self.z_parts = self.in_half * cores
        self.nz = half_z // self.in_half
        self.rows = nx // QUARTERS
        self.main = self.rows // TILE
        self.tiles = self.main + 1
        self.ext = self.nz + 2 * GHOST
        self.sides = 1 if self.z_parts == 2 else 2
        self.z_tiles = GHOST * self.main + GHOST - 1
        self.raw_tiles = GHOST * self.tiles * RAW
        kinds = [(2, 0), (1, 0), (1, 1), (0, 1), (2, 1), (3, 0), (3, 1), (0, 0)]
        self.rounds = [a * self.per_quarter + m * 2 + c for m in range(self.in_half) for a, c in kinds]

        self.back, self.ties = self.return_order()

    def return_order(self):
        pieces = len(self.pieces())
        near = [r for r in self.rounds if self.direct(r)]
        far = [r for r in self.rounds if not self.direct(r)]
        if pieces == 1:
            return [[(r, None) for r in far + near]], ()
        far = far[2:] + far[:2]
        back = [[(r, 0) for r in far], [(r, 1) for r in far] + [(r, None) for r in near]]
        return back, [(2 * len(far) + n, len(far) - 1) for n in range(len(near) - 1)]

    def pieces(self):
        if self.sides == 1 and self.nz >= 4 * GHOST:
            return [self.nz // 2, self.nz // 2]
        return [self.nz]

    def layers(self, piece):
        return self.nz if piece is None else self.pieces()[piece]

    def direct(self, r):
        return r // self.per_quarter < 2

    def stride(self, r):
        return self.rows + TILE if self.direct(r) else self.rows

    def pairs(self, r):
        return [(i, i ^ r) for i in range(self.steps)]

    def x_pairs(self, first):
        result = []
        for hi in range(first, QUARTERS - 1, 2):
            for lo in range(self.per_quarter):
                one = hi * self.per_quarter + lo
                result += [(one, one + self.per_quarter), (one + self.per_quarter, one)]
        return result

    def z_pairs(self, first):
        def flat(hi, zb, part):
            return (hi * self.per_quarter + zb % self.in_half * 2 + part) * self.cores + zb // self.in_half

        result = []
        for zb in range(first, self.z_parts - 1, 2):
            for hi in range(QUARTERS):
                for part in range(2):
                    one, two = flat(hi, zb, part), flat(hi, zb + 1, part)
                    result += [(one, two), (two, one)]
        return result


class Place:
    def __init__(self, plan, ref):
        self.t, self.s = ref[0], ref[1]
        self.hi, self.lo = self.t // plan.per_quarter, self.t % plan.per_quarter
        self.zm, self.part = self.lo // 2, self.lo % 2
        self.zb = self.s * plan.in_half + self.zm
        self.hi_odd, self.zb_odd = self.hi % 2 == 1, self.zb % 2 == 1
        self.up = self.zb == 0

    def piece(self, plan, number):
        sizes = plan.pieces()
        before = sum(sizes[:number])
        if len(sizes) == 1:
            return 0
        return jnp.where(self.up, before, plan.nz - before - sizes[number])


def kernel_call(body, outs, args, scratch=(), spaces=None, out_space=pltpu.VMEM, limit=16, aliases=None):
    spaces = [pltpu.SMEM] + (spaces or [pltpu.VMEM] * (len(args) - 1))
    single = isinstance(outs, tuple)
    shapes = [outs] if single else list(outs)
    result = pl.pallas_call(
        body,
        out_shape=[jax.ShapeDtypeStruct(s, jnp.float32) for s in shapes],
        in_specs=[pl.BlockSpec(memory_space=space) for space in spaces],
        out_specs=[pl.BlockSpec(memory_space=out_space)] * len(shapes),
        scratch_shapes=list(scratch),
        input_output_aliases=aliases or {},
        compiler_params=pltpu.CompilerParams(vmem_limit_bytes=limit << 20),
    )(*args)
    return result[0] if single else result


def rows_at(index, count=1):
    return pl.ds(pl.multiple_of(index * TILE, TILE), count * TILE)


def sublane(plan):
    return lax.broadcasted_iota(jnp.int32, (TILE, plan.ny), 0)


def lane(plan):
    return lax.broadcasted_iota(jnp.int32, (TILE, plan.ny), 1)


def near_tiles(plan, hi):
    per = plan.nx // TILE
    own = [hi * plan.main + k for k in range(plan.main)]
    return own, jnp.minimum(own[-1] + 1, per - 1), jnp.maximum(own[0] - 1, 0)


def write_coefs(plan, hi, inside, k, values, store):
    row, col = sublane(plan), lane(plan)
    d, vz, vx, vy = values
    if k < plan.main:
        x = row + k * TILE
    else:
        x = jnp.where(row < GHOST, row + plan.rows, row - TILE)
    x = x + hi * plan.rows
    keep = (x >= 0) & (x < plan.nx)
    if k == plan.main:
        keep = keep & ((row < GHOST) | (row >= TILE - GHOST))
    if inside is not None:
        keep = keep & inside
    total = inv_step + 6.0 * d + (jnp.abs(vz) + jnp.abs(vx) + jnp.abs(vy))
    w = jnp.where(keep, 1.0 / total, 0.0)
    c = inv_step * w
    power = c
    for _ in range(plan.steps.bit_length() - 1):
        power = power * power
    wrap = alpha_circ / (1.0 - alpha_circ * power)
    low = [w * (d + jnp.maximum(v, 0.0)) for v in (vz, vx, vy)]
    high = [w * (d + jnp.maximum(-v, 0.0)) for v in (vz, vx, vy)]
    low[2] = jnp.where(col == 0, 0.0, low[2])
    high[2] = jnp.where(col == plan.ny - 1, 0.0, high[2])
    for n, value in enumerate([w, c, wrap] + low + high):
        store(n, value)


def make_coefs(plan, place_ref, d_ref, v_ref, out_ref, *raw_refs):
    place = Place(plan, place_ref)
    per = plan.nx // TILE
    row = sublane(plan)
    own, over, under = near_tiles(plan, place.hi)

    def read(z):
        z = place.zm * plan.nz + z
        found = []
        for n in range(RAW):
            ref, base = (d_ref, z * per) if n == 0 else (v_ref, ((n - 1) * plan.half_z + z) * per)
            edge = jnp.where(row < TILE // 2, ref[rows_at(base + over), :], ref[rows_at(base + under), :])
            found.append([ref[rows_at(base + at), :] for at in own] + [edge])
        return [[tiles[k] for tiles in found] for k in range(plan.tiles)]

    def layer(z, _):
        for k, values in enumerate(read(z)):

            def store(n, value, k=k):
                out_ref[rows_at(((z + GHOST) * plan.tiles + k) * COEFS + n), :] = value

            write_coefs(plan, place.hi, None, k, values, store)
        return 0

    lax.fori_loop(0, plan.nz, layer, 0)
    for side, raw in enumerate(raw_refs):
        up = jnp.logical_not(place.zb_odd) if side == 0 else place.zb_odd
        for n in range(GHOST):
            for k, values in enumerate(read(jnp.where(up, plan.nz - GHOST + n, n))):
                for at, value in enumerate(values):
                    raw[rows_at((n * plan.tiles + k) * RAW + at), :] = value


def pack_blocks(plan, rounds, place_ref, right, *outs):
    place = Place(plan, place_ref)
    per = plan.nx // TILE
    row = sublane(plan)
    for out, r in zip(outs, rounds):
        target = place.t ^ r
        quarter, lo = target // plan.per_quarter, target % plan.per_quarter
        first = lo % 2 * plan.half_z + lo // 2 * plan.nz
        own, over, under = near_tiles(plan, quarter)
        tiles = plan.stride(r) // TILE
        for z in range(plan.nz):
            base = (first + z) * per
            for k, at in enumerate(own):
                out[rows_at(z * tiles + k), :] = right[rows_at(base + at), :]
            if plan.direct(r):
                edge = jnp.where(row < TILE // 2, right[rows_at(base + over), :], right[rows_at(base + under), :])
                out[rows_at(z * tiles + plan.main), :] = edge


def edge_rows(plan, place_ref, *refs):
    place = Place(plan, place_ref)
    blocks, (x_even, x_odd) = refs[: plan.steps], refs[plan.steps :]
    half = plan.steps // 2
    for block, r in zip(blocks, plan.rounds):
        step = (place.t ^ r) % half
        stride = plan.stride(r)
        for n in range(GHOST):
            low = block[pl.ds(n, plan.nz, stride=stride), :]
            high = block[pl.ds(plan.rows - GHOST + n, plan.nz, stride=stride), :]
            at = pl.ds((n * half + step) * plan.nz, plan.nz)
            if plan.direct(r):
                x_odd[at, :] = jnp.where(place.hi_odd, high, low)
            else:
                x_even[at, :] = jnp.where(place.hi_odd, low, high)


def gather_steps(plan, place_ref, *refs):
    place = Place(plan, place_ref)
    blocks, field = refs[: plan.steps], refs[plan.steps]
    size = plan.nz * plan.rows
    for block, r in zip(blocks, plan.rounds):
        at = (place.t ^ r) * size
        for z in range(plan.nz):
            to = pl.ds(pl.multiple_of(at + z * plan.rows, TILE), plan.rows)
            field[to, :] = block[pl.ds(z * plan.stride(r), plan.rows), :]


def gather_ghosts(plan, place_ref, field, even_ref, odd_ref, *refs):
    place = Place(plan, place_ref)
    direct = [r for r in plan.rounds if plan.direct(r)]
    blocks, refs = refs[: len(direct)], refs[len(direct) :]
    raws, refs = refs[: plan.sides], refs[plan.sides :]
    ghost, z_sends, planes = refs[0], refs[1:-1], refs[-1]
    half = plan.steps // 2
    count = half * plan.nz
    for block, r in zip(blocks, direct):
        at = (place.t ^ r) * plan.nz
        for z in range(plan.nz):
            ghost[rows_at(at + z), :] = block[pl.ds(z * plan.stride(r) + plan.rows, TILE), :]
    for n in range(GHOST):
        even, odd = even_ref[pl.ds(n * count, count), :], odd_ref[pl.ds(n * count, count), :]
        planes[pl.ds(n * count, count), :] = jnp.where(place.hi_odd, odd, even)
        planes[pl.ds((TILE - GHOST + n) * count, count), :] = jnp.where(place.hi_odd, even, odd)
    for n in range(GHOST, TILE - GHOST):
        planes[pl.ds(n * count, count), :] = jnp.zeros((count, plan.ny), jnp.float32)
    first = (1 - place.hi // 2) * count
    for n in range(count):
        ghost[rows_at(first + n), :] = planes[pl.ds(n, TILE, stride=count), :]
    deep, tiles = GHOST - 1, plan.z_tiles
    for side, (raw, z_send) in enumerate(zip(raws, z_sends)):
        up = jnp.logical_not(place.zb_odd) if side == 0 else place.zb_odd
        for t in range(plan.steps):
            for n in range(GHOST):
                z = t * plan.nz + jnp.where(up, plan.nz - GHOST + n, n)
                for k in range(plan.main):
                    z_send[rows_at(t * tiles + n * plan.main + k), :] = field[rows_at(z * plan.main + k), :]
            for n in range(deep):
                z = t * plan.nz + jnp.where(up, plan.nz - deep + n, n)
                z_send[rows_at(t * tiles + GHOST * plan.main + n), :] = ghost[rows_at(z), :]
        z_send[rows_at(plan.steps * tiles, plan.raw_tiles), :] = raw[...]


class Sweeps:
    def __init__(self, plan, place, coefs, source, ping, pong, last):
        self.plan, self.coefs = plan, coefs
        self.source, self.buffers, self.last = source, (ping, pong), last
        self.has_low, self.has_high = place.zb > 0, place.zb < plan.z_parts - 1
        self.low_at, self.high_at = GHOST, GHOST + plan.nz

    def spot(self, e, k, t):
        return rows_at((e * self.plan.tiles + k) * self.plan.steps + t)

    def coef(self, e, k, n):
        return self.coefs[rows_at((e * self.plan.tiles + k) * COEFS + n), :]

    def first(self, e, k, values):
        w, c, wrap = (self.coef(e, k, n) for n in range(3))
        partial = []
        for t, value in enumerate(values):
            value = w * value
            self.source[self.spot(e, k, t), :] = value
            if t:
                value = value + c * partial[-1]
            partial.append(value)
        carry = c * (wrap * partial[-1])
        for t, value in enumerate(partial):
            self.buffers[0][self.spot(e, k, t), :] = value + carry
            carry = c * carry

    def sweep(self, number, start, stop, total=None):
        plan, steps, tiles, ny = self.plan, self.plan.steps, self.plan.tiles, self.plan.ny
        old, new = self.buffers[(number - 1) % 2], self.buffers[number % 2]
        final = number == SWEEPS - 1
        wide = plan.main if final else tiles
        row = sublane(plan)
        spot, coef = self.spot, self.coef

        def layers(e, count):
            parts = [(e + g, k) for g in range(count) for k in range(wide)]
            c = [coef(at, k, 1) for at, k in parts]
            near = [[coef(at, k, n) for n in range(3, COEFS)] for at, k in parts]
            partial = [[] for _ in parts]
            for g in range(count):
                at = e + g
                for t in range(steps):
                    here = [old[spot(at, k, t), :] for k in range(tiles)]
                    down = [pltpu.roll(value, 1, 0) for value in here]
                    up = [pltpu.roll(value, TILE - 1, 0) for value in here]
                    for k in range(wide):
                        n = g * wide + k
                        z_low, x_low, y_low, z_high, x_high, y_high = near[n]
                        below = jnp.where(row == 0, down[k - 1], down[k])
                        above = jnp.where(row == TILE - 1, up[(k + 1) % tiles], up[k])
                        total = self.source[spot(at, k, t), :] + z_low * old[spot(at - 1, k, t), :]
                        total = total + z_high * old[spot(at + 1, k, t), :]
                        total = total + (x_low * below + x_high * above)
                        total = total + (
                            y_low * pltpu.roll(here[k], 1, 1) + y_high * pltpu.roll(here[k], ny - 1, 1)
                        )
                        if t:
                            total = total + c[n] * partial[n][-1]
                        partial[n].append(total)
            for n, (at, k) in enumerate(parts):
                carry = c[n] * (coef(at, k, 2) * partial[n][-1])
                for t in range(steps):
                    value = partial[n][t] + carry
                    carry = c[n] * carry
                    if final:
                        self.last[rows_at((t * plan.nz + at - GHOST) * plan.main + k), :] = value
                    else:
                        new[spot(at, k, t), :] = value

        if total is not None:

            def several(i, _):
                layers(start + i * GROUP, GROUP)
                return 0

            lax.fori_loop(0, total // GROUP, several, 0)
            if total % GROUP:
                layers(start + total // GROUP * GROUP, total % GROUP)
        else:

            def one(e, _):
                layers(e, 1)
                return 0

            lax.fori_loop(start, stop, one, 0)


def first_pass(plan, work, field, ghost, start, count):
    steps, main = plan.steps, plan.main

    def layer(z):
        for k in range(main):
            work.first(z + GHOST, k, [field[rows_at((t * plan.nz + z) * main + k), :] for t in range(steps)])
        work.first(z + GHOST, main, [ghost[rows_at(t * plan.nz + z), :] for t in range(steps)])

    def several(i, _):
        for n in range(4):
            layer(start + i * 4 + n)
        return 0

    lax.fori_loop(0, count // 4, several, 0)
    for n in range(count // 4 * 4, count):
        layer(start + n)


def ghost_pass(plan, place, work, z_in):
    steps, main, sides, deep = plan.steps, plan.main, plan.sides, GHOST - 1
    coefs, source, ping = work.coefs, work.source, work.buffers[0]
    empty = jnp.zeros((TILE, plan.ny), jnp.float32)

    def ghost_layers(at, upper, z_ref):
        for n in range(GHOST):
            e = at + n
            for k in range(plan.tiles):
                raw = steps * plan.z_tiles + (n * plan.tiles + k) * RAW

                def store(number, value, k=k, e=e):
                    coefs[rows_at((e * plan.tiles + k) * COEFS + number), :] = value

                write_coefs(plan, place.hi, None, k, [z_ref[rows_at(raw + m), :] for m in range(RAW)], store)
            for k in range(main):
                tile = n * main + k
                work.first(e, k, [z_ref[rows_at(t * plan.z_tiles + tile), :] for t in range(steps)])
            c_at = n if upper else n - (GHOST - deep)
            if 0 <= c_at < deep:
                tile = GHOST * main + c_at
                work.first(e, main, [z_ref[rows_at(t * plan.z_tiles + tile), :] for t in range(steps)])
            else:
                for t in range(steps):
                    ping[work.spot(e, main, t), :] = empty
                    source[work.spot(e, main, t), :] = empty

    for odd in (False, True):

        @pl.when(work.has_low & (place.zb_odd == odd))
        def _(odd=odd):
            ghost_layers(0, False, z_in[0 if odd else sides - 1])

        @pl.when(work.has_high & (place.zb_odd == odd))
        def _(odd=odd):
            ghost_layers(work.high_at, True, z_in[sides - 1 if odd else 0])


def no_ghosts(plan, work):
    empty = jnp.zeros((TILE, plan.ny), jnp.float32)
    for outside, e in ((work.has_low, work.low_at - 1), (work.has_high, work.high_at)):

        @pl.when(jnp.logical_not(outside))
        def _(e=e):
            for k in range(plan.tiles):
                for t in range(plan.steps):
                    for buffer in work.buffers:
                        buffer[work.spot(e, k, t), :] = empty


def write_piece(plan, place, last, outs, number):
    for out, (r, piece) in zip(outs, plan.back[number]):
        start = 0 if piece is None else place.piece(plan, piece)
        at = ((place.t ^ r) * plan.nz + start) * plan.rows
        out[...] = last[pl.ds(pl.multiple_of(at, TILE), out.shape[0]), :]


def all_sweeps(plan, place_ref, coefs_in, field, ghost, *refs):
    place = Place(plan, place_ref)
    z_in, refs = refs[: plan.sides], refs[plan.sides :]
    outs, (coefs, source, ping, pong, last) = refs[:-5], refs[-5:]
    work = Sweeps(plan, place, coefs, source, ping, pong, last)
    first_pass(plan, work, field, ghost, 0, plan.nz)
    ghost_pass(plan, place, work, z_in)
    no_ghosts(plan, work)
    for number in range(1, SWEEPS):
        reach = SWEEPS - 1 - number
        start = work.low_at - jnp.where(work.has_low, reach, 0)
        stop = work.high_at + jnp.where(work.has_high, reach, 0)
        work.sweep(number, start, stop)
    write_piece(plan, place, last, outs, 0)


def far_sweeps(plan, place_ref, coefs, field, ghost, *refs):
    place = Place(plan, place_ref)
    outs, (source, ping, pong, last) = refs[:-4], refs[-4:]
    work = Sweeps(plan, place, coefs, source, ping, pong, last)
    count = plan.pieces()[0]
    first_pass(plan, work, field, ghost, jnp.where(place.up, 0, plan.nz - count - GHOST), count + GHOST)
    no_ghosts(plan, work)
    for number in range(1, SWEEPS):
        total = count + SWEEPS - 1 - number
        start = jnp.where(place.up, work.low_at, work.high_at - total)
        work.sweep(number, start, start + total, total)
    write_piece(plan, place, last, outs, 0)


def near_sweeps(plan, place_ref, field, ghost, z_in, coefs_in, source_in, ping_in, pong_in, last_in, *refs):
    place = Place(plan, place_ref)
    outs, (coefs, source, ping, pong, last) = refs[:-5], refs[-5:]
    work = Sweeps(plan, place, coefs, source, ping, pong, last)
    first, count = plan.pieces()
    left = plan.nz - first - GHOST
    first_pass(plan, work, field, ghost, jnp.where(place.up, plan.nz - left, 0), left)
    ghost_pass(plan, place, work, [z_in])
    for number in range(1, SWEEPS):
        reach = SWEEPS - 1 - number
        start = jnp.where(place.up, work.low_at + first + reach, work.low_at - reach)
        work.sweep(number, start, start + count, count)
    write_piece(plan, place, last, outs, 1)


def run_sweeps(plan, call, coefs, field, ghost, z_of):
    grid = (plan.ext * plan.tiles * plan.steps * TILE, plan.ny)
    whole = (plan.steps * plan.nz * plan.rows, plan.ny)
    shapes = [[(plan.layers(piece) * plan.rows, plan.ny) for r, piece in blocks] for blocks in plan.back]
    if len(shapes) == 1:
        scratch = [pltpu.VMEM(shape, jnp.float32) for shape in [grid] * 3 + [whole]]
        inputs = (coefs, field, ghost, *z_of())
        found = call(
            all_sweeps, shapes[0] + [coefs.shape], inputs, scratch=scratch, aliases={1: len(shapes[0])}, limit=24
        )
        return [found[:-1]]
    *done, source, ping, pong, last = call(
        far_sweeps, shapes[0] + [grid] * 3 + [whole], (coefs, field, ghost), limit=24
    )
    rest = call(
        near_sweeps,
        shapes[1] + [coefs.shape] + [grid] * 3 + [whole],
        (field, ghost, *z_of(), coefs, source, ping, pong, last),
        aliases={4 + n: len(shapes[1]) + n for n in range(5)},
        limit=24,
    )
    return [done, rest[:-5]]


def place_blocks(plan, place_ref, *refs):
    place = Place(plan, place_ref)
    blocks, (out, sems) = refs[:-2], refs[-2:]
    copies = []
    for n, (block, (r, piece)) in enumerate(zip(blocks, sum(plan.back, []))):
        source = place.t ^ r
        quarter, lo = source // plan.per_quarter, source % plan.per_quarter
        z = lo // 2 * plan.nz + (0 if piece is None else place.piece(plan, piece))
        x = pl.multiple_of(quarter * plan.rows, plan.rows)
        target = out.at[lo % 2, pl.ds(z, plan.layers(piece)), pl.ds(x, plan.rows), :]
        copies.append(pltpu.make_async_copy(block, target, sems.at[n]))
    for copy in copies:
        copy.start()
    for copy in copies:
        copy.wait()


def local(right_side, diffusivity, velocity):
    steps, cores = lax.axis_size("tm"), lax.axis_size("space")
    _, parts, half_z, nx, ny = right_side.shape
    plan = Plan(steps, cores, half_z, nx, ny)
    place = jnp.stack([lax.axis_index("tm"), lax.axis_index("space")]).astype(jnp.int32)
    size = plan.nz * plan.rows
    half_x = steps // 2 * plan.nz

    def call(body, outs, arrays, extra=None, **options):
        body = functools.partial(body, plan) if extra is None else functools.partial(body, plan, extra)
        return kernel_call(body, outs, (place, *arrays), **options)

    def turned(arrays, rounds, ties=(), known=()):
        found = list(known)
        for n, (array, r) in enumerate(zip(arrays, rounds), len(found)):
            for late, early in ties:
                if n == late:
                    array, found[early] = lax.optimization_barrier((array, found[early]))
            found.append(array if r == 0 else lax.ppermute(array, "tm", plan.pairs(r)))
        return found

    sends = call(
        pack_blocks,
        [(plan.nz * plan.stride(r), ny) for r in plan.rounds],
        (right_side.reshape(parts * half_z * nx, ny),),
        extra=plan.rounds,
    )
    blocks = turned(sends, plan.rounds)
    blocks = lax.optimization_barrier(blocks)
    x_even, x_odd = call(edge_rows, [(GHOST * half_x, ny)] * 2, blocks)
    even = lax.ppermute(x_even, "tm", plan.x_pairs(0))
    odd = lax.ppermute(x_odd, "tm", plan.x_pairs(1))
    diffusivity, velocity, *blocks = lax.optimization_barrier((diffusivity, velocity, *blocks))
    field = call(gather_steps, (steps * size, ny), blocks)
    coefs, *raws = call(
        make_coefs,
        [(plan.ext * plan.tiles * COEFS * TILE, ny)] + [(plan.raw_tiles * TILE, ny)] * plan.sides,
        (diffusivity.reshape(half_z * nx, ny), velocity.reshape(3 * half_z * nx, ny)),
    )
    direct = [block for block, r in zip(blocks, plan.rounds) if plan.direct(r)]
    ghost, *z_sends = call(
        gather_ghosts,
        [(steps * plan.nz * TILE, ny)] + [((steps * plan.z_tiles + plan.raw_tiles) * TILE, ny)] * plan.sides,
        (field, even, odd, *direct, *raws),
        scratch=[pltpu.VMEM((half_x * TILE, ny), jnp.float32)],
    )

    def z_of():
        return [lax.ppermute(send, FLAT, plan.z_pairs(first)) for first, send in enumerate(z_sends)]

    solved = run_sweeps(plan, call, coefs, field, ghost, z_of)
    back = []
    for found, blocks in zip(solved, plan.back):
        back = turned(found, [r for r, piece in blocks], plan.ties, back)
    back = [
        block.reshape(plan.layers(piece), plan.rows, ny) for block, (r, piece) in zip(back, sum(plan.back, []))
    ]
    out = call(
        place_blocks,
        (parts, half_z, nx, ny),
        back,
        scratch=[pltpu.SemaphoreType.DMA((len(back),))],
        out_space=pltpu.HBM,
    )
    return out[None]


def solution(mesh):
    placed = (
        P(("group", "tm"), None, "space", None, None),
        P("space", None, None),
        P(None, "space", None, None),
    )
    return jax.shard_map(
        local,
        mesh=mesh,
        in_specs=placed,
        out_specs=P(("group", "tm"), None, "space", None, None),
        check_vma=False,
    )
```

```python
import functools

import jax
import jax.numpy as jnp
from jax import lax
from jax.experimental import pallas as pl
from jax.experimental.pallas import tpu as pltpu
from jax.sharding import PartitionSpec as P

SWEEPS = 4
GHOST = SWEEPS - 1
QUARTERS = 4
TILE = 8
COEFS = 9
RAW = 4
GROUP = 6

alpha_circ = 0.1
inv_step = 2.0

FLAT = ("tm", "space")


class Plan:
    def __init__(self, steps, cores, half_z, nx, ny):
        self.steps, self.cores, self.half_z, self.nx, self.ny = steps, cores, half_z, nx, ny
        self.per_quarter = steps // QUARTERS
        self.in_half = self.per_quarter // 2
        self.z_parts = self.in_half * cores
        self.nz = half_z // self.in_half
        self.rows = nx // QUARTERS
        self.main = self.rows // TILE
        self.tiles = self.main + 1
        self.ext = self.nz + 2 * GHOST
        self.sides = 1 if self.z_parts == 2 else 2
        self.z_tiles = GHOST * self.main + GHOST - 1
        self.raw_tiles = GHOST * self.tiles * RAW
        self.ghost_inputs = 2 + steps // 2 + self.sides
        kinds = [(2, 0), (1, 0), (1, 1), (0, 1), (2, 1), (3, 0), (3, 1), (0, 0)]
        self.rounds = [a * self.per_quarter + m * 2 + c for m in range(self.in_half) for a, c in kinds]

        self.back, self.ties = self.return_order()

    def return_order(self):
        pieces = len(self.pieces())
        near = [r for r in self.rounds if self.direct(r)]
        far = [r for r in self.rounds if not self.direct(r)]
        if pieces == 1:
            return [[(r, None) for r in far + near]], ()
        far = far[2:] + far[:2]
        back = [[(r, 0) for r in far], [(r, 1) for r in far] + [(r, None) for r in near]]
        return back, [(2 * len(far) + n, len(far) - 1) for n in range(len(near) - 1)]

    def pieces(self):
        if self.sides == 1 and self.nz >= 4 * GHOST:
            return [self.nz // 2, self.nz // 2]
        return [self.nz]

    def layers(self, piece):
        return self.nz if piece is None else self.pieces()[piece]

    def direct(self, r):
        return r // self.per_quarter < 2

    def stride(self, r):
        return self.rows + TILE if self.direct(r) else self.rows

    def pairs(self, r):
        return [(i, i ^ r) for i in range(self.steps)]

    def x_pairs(self, first):
        result = []
        for hi in range(first, QUARTERS - 1, 2):
            for lo in range(self.per_quarter):
                one = hi * self.per_quarter + lo
                result += [(one, one + self.per_quarter), (one + self.per_quarter, one)]
        return result

    def z_pairs(self, first):
        def flat(hi, zb, part):
            return (hi * self.per_quarter + zb % self.in_half * 2 + part) * self.cores + zb // self.in_half

        result = []
        for zb in range(first, self.z_parts - 1, 2):
            for hi in range(QUARTERS):
                for part in range(2):
                    one, two = flat(hi, zb, part), flat(hi, zb + 1, part)
                    result += [(one, two), (two, one)]
        return result


class Place:
    def __init__(self, plan, ref):
        self.t, self.s = ref[0], ref[1]
        self.hi, self.lo = self.t // plan.per_quarter, self.t % plan.per_quarter
        self.zm, self.part = self.lo // 2, self.lo % 2
        self.zb = self.s * plan.in_half + self.zm
        self.hi_odd, self.zb_odd = self.hi % 2 == 1, self.zb % 2 == 1
        self.up = self.zb == 0

    def piece(self, plan, number):
        sizes = plan.pieces()
        before = sum(sizes[:number])
        if len(sizes) == 1:
            return 0
        return jnp.where(self.up, before, plan.nz - before - sizes[number])


def kernel_call(body, outs, args, scratch=(), spaces=None, out_space=pltpu.VMEM, limit=16, aliases=None):
    spaces = [pltpu.SMEM] + (spaces or [pltpu.VMEM] * (len(args) - 1))
    single = isinstance(outs, tuple)
    shapes = [outs] if single else list(outs)
    result = pl.pallas_call(
        body,
        out_shape=[jax.ShapeDtypeStruct(s, jnp.float32) for s in shapes],
        in_specs=[pl.BlockSpec(memory_space=space) for space in spaces],
        out_specs=[pl.BlockSpec(memory_space=out_space)] * len(shapes),
        scratch_shapes=list(scratch),
        input_output_aliases=aliases or {},
        compiler_params=pltpu.CompilerParams(vmem_limit_bytes=limit << 20),
    )(*args)
    return result[0] if single else result


def rows_at(index, count=1):
    return pl.ds(pl.multiple_of(index * TILE, TILE), count * TILE)


def sublane(plan):
    return lax.broadcasted_iota(jnp.int32, (TILE, plan.ny), 0)


def lane(plan):
    return lax.broadcasted_iota(jnp.int32, (TILE, plan.ny), 1)


def near_tiles(plan, hi):
    per = plan.nx // TILE
    own = [hi * plan.main + k for k in range(plan.main)]
    return own, jnp.minimum(own[-1] + 1, per - 1), jnp.maximum(own[0] - 1, 0)


def write_coefs(plan, hi, inside, k, values, store):
    row, col = sublane(plan), lane(plan)
    d, vz, vx, vy = values
    if k < plan.main:
        x = row + k * TILE
    else:
        x = jnp.where(row < GHOST, row + plan.rows, row - TILE)
    x = x + hi * plan.rows
    keep = (x >= 0) & (x < plan.nx)
    if k == plan.main:
        keep = keep & ((row < GHOST) | (row >= TILE - GHOST))
    if inside is not None:
        keep = keep & inside
    total = inv_step + 6.0 * d + (jnp.abs(vz) + jnp.abs(vx) + jnp.abs(vy))
    w = jnp.where(keep, 1.0 / total, 0.0)
    c = inv_step * w
    power = c
    for _ in range(plan.steps.bit_length() - 1):
        power = power * power
    wrap = alpha_circ / (1.0 - alpha_circ * power)
    low = [w * (d + jnp.maximum(v, 0.0)) for v in (vz, vx, vy)]
    high = [w * (d + jnp.maximum(-v, 0.0)) for v in (vz, vx, vy)]
    low[2] = jnp.where(col == 0, 0.0, low[2])
    high[2] = jnp.where(col == plan.ny - 1, 0.0, high[2])
    for n, value in enumerate([w, c, wrap] + low + high):
        store(n, value)


def make_coefs(plan, place_ref, d_ref, v_ref, out_ref, *raw_refs):
    place = Place(plan, place_ref)
    per = plan.nx // TILE
    row = sublane(plan)
    own, over, under = near_tiles(plan, place.hi)

    def read(z):
        z = place.zm * plan.nz + z
        found = []
        for n in range(RAW):
            ref, base = (d_ref, z * per) if n == 0 else (v_ref, ((n - 1) * plan.half_z + z) * per)
            edge = jnp.where(row < TILE // 2, ref[rows_at(base + over), :], ref[rows_at(base + under), :])
            found.append([ref[rows_at(base + at), :] for at in own] + [edge])
        return [[tiles[k] for tiles in found] for k in range(plan.tiles)]

    def layer(z, _):
        for k, values in enumerate(read(z)):

            def store(n, value, k=k):
                out_ref[rows_at(((z + GHOST) * plan.tiles + k) * COEFS + n), :] = value

            write_coefs(plan, place.hi, None, k, values, store)
        return 0

    lax.fori_loop(0, plan.nz, layer, 0)
    for side, raw in enumerate(raw_refs):
        up = jnp.logical_not(place.zb_odd) if side == 0 else place.zb_odd
        for n in range(GHOST):
            for k, values in enumerate(read(jnp.where(up, plan.nz - GHOST + n, n))):
                for at, value in enumerate(values):
                    raw[rows_at((n * plan.tiles + k) * RAW + at), :] = value


def pack_blocks(plan, rounds, place_ref, right, *outs):
    place = Place(plan, place_ref)
    per = plan.nx // TILE
    row = sublane(plan)
    for out, r in zip(outs, rounds):
        target = place.t ^ r
        quarter, lo = target // plan.per_quarter, target % plan.per_quarter
        first = lo % 2 * plan.half_z + lo // 2 * plan.nz
        own, over, under = near_tiles(plan, quarter)
        tiles = plan.stride(r) // TILE
        for z in range(plan.nz):
            base = (first + z) * per
            for k, at in enumerate(own):
                out[rows_at(z * tiles + k), :] = right[rows_at(base + at), :]
            if plan.direct(r):
                edge = jnp.where(row < TILE // 2, right[rows_at(base + over), :], right[rows_at(base + under), :])
                out[rows_at(z * tiles + plan.main), :] = edge


def edge_rows(plan, place_ref, *refs):
    place = Place(plan, place_ref)
    blocks, (x_even, x_odd) = refs[: plan.steps], refs[plan.steps :]
    half = plan.steps // 2
    for block, r in zip(blocks, plan.rounds):
        step = (place.t ^ r) % half
        stride = plan.stride(r)
        for n in range(GHOST):
            low = block[pl.ds(n, plan.nz, stride=stride), :]
            high = block[pl.ds(plan.rows - GHOST + n, plan.nz, stride=stride), :]
            at = pl.ds((n * half + step) * plan.nz, plan.nz)
            if plan.direct(r):
                x_odd[at, :] = jnp.where(place.hi_odd, high, low)
            else:
                x_even[at, :] = jnp.where(place.hi_odd, low, high)


def first_own(plan, place_ref, coefs, *refs):
    place = Place(plan, place_ref)
    blocks, (source, ping, field) = refs[: plan.steps], refs[plan.steps :]
    size = plan.nz * plan.rows
    for block, r in zip(blocks, plan.rounds):
        at = (place.t ^ r) * size
        for z in range(plan.nz):
            to = pl.ds(pl.multiple_of(at + z * plan.rows, TILE), plan.rows)
            field[to, :] = block[pl.ds(z * plan.stride(r), plan.rows), :]
    work = Sweeps(plan, place, coefs, source, ping, None, None)

    def several(i, _):
        for n in range(4):
            z = i * 4 + n
            for k in range(plan.main):
                tiles = [field[rows_at((t * plan.nz + z) * plan.main + k), :] for t in range(plan.steps)]
                work.first(z + GHOST, k, tiles)
        return 0

    lax.fori_loop(0, plan.nz // 4, several, 0)


def gather_ghosts(plan, place_ref, source, even_ref, odd_ref, *refs):
    place = Place(plan, place_ref)
    direct = [r for r in plan.rounds if plan.direct(r)]
    blocks, refs = refs[: len(direct)], refs[len(direct) :]
    raws, refs = refs[: plan.sides], refs[plan.sides :]
    ghost, z_sends, planes = refs[0], refs[1:-1], refs[-1]
    half = plan.steps // 2
    count = half * plan.nz
    for block, r in zip(blocks, direct):
        at = (place.t ^ r) * plan.nz
        for z in range(plan.nz):
            ghost[rows_at(at + z), :] = block[pl.ds(z * plan.stride(r) + plan.rows, TILE), :]
    for n in range(GHOST):
        even, odd = even_ref[pl.ds(n * count, count), :], odd_ref[pl.ds(n * count, count), :]
        planes[pl.ds(n * count, count), :] = jnp.where(place.hi_odd, odd, even)
        planes[pl.ds((TILE - GHOST + n) * count, count), :] = jnp.where(place.hi_odd, even, odd)
    for n in range(GHOST, TILE - GHOST):
        planes[pl.ds(n * count, count), :] = jnp.zeros((count, plan.ny), jnp.float32)
    first = (1 - place.hi // 2) * count
    for n in range(count):
        ghost[rows_at(first + n), :] = planes[pl.ds(n, TILE, stride=count), :]
    deep, tiles = GHOST - 1, plan.z_tiles
    for side, (raw, z_send) in enumerate(zip(raws, z_sends)):
        up = jnp.logical_not(place.zb_odd) if side == 0 else place.zb_odd
        for t in range(plan.steps):
            for n in range(GHOST):
                e = GHOST + jnp.where(up, plan.nz - GHOST + n, n)
                for k in range(plan.main):
                    to = rows_at(t * tiles + n * plan.main + k)
                    z_send[to, :] = source[rows_at((e * plan.tiles + k) * plan.steps + t), :]
            for n in range(deep):
                z = t * plan.nz + jnp.where(up, plan.nz - deep + n, n)
                z_send[rows_at(t * tiles + GHOST * plan.main + n), :] = ghost[rows_at(z), :]
        z_send[rows_at(plan.steps * tiles, plan.raw_tiles), :] = raw[...]


class Sweeps:
    def __init__(self, plan, place, coefs, source, ping, pong, last):
        self.plan, self.coefs = plan, coefs
        self.source, self.buffers, self.last = source, (ping, pong), last
        self.has_low, self.has_high = place.zb > 0, place.zb < plan.z_parts - 1
        self.low_at, self.high_at = GHOST, GHOST + plan.nz

    def spot(self, e, k, t):
        return rows_at((e * self.plan.tiles + k) * self.plan.steps + t)

    def coef(self, e, k, n):
        return self.coefs[rows_at((e * self.plan.tiles + k) * COEFS + n), :]

    def first(self, e, k, values, scaled=False):
        w, c, wrap = (self.coef(e, k, n) for n in range(3))
        partial = []
        for t, value in enumerate(values):
            value = value if scaled else w * value
            self.source[self.spot(e, k, t), :] = value
            if t:
                value = value + c * partial[-1]
            partial.append(value)
        carry = c * (wrap * partial[-1])
        for t, value in enumerate(partial):
            self.buffers[0][self.spot(e, k, t), :] = value + carry
            carry = c * carry

    def sweep(self, number, start, stop, total=None):
        plan, steps, tiles, ny = self.plan, self.plan.steps, self.plan.tiles, self.plan.ny
        old, new = self.buffers[(number - 1) % 2], self.buffers[number % 2]
        final = number == SWEEPS - 1
        wide = plan.main if final else tiles
        row = sublane(plan)
        spot, coef = self.spot, self.coef

        def layers(e, count):
            parts = [(e + g, k) for g in range(count) for k in range(wide)]
            c = [coef(at, k, 1) for at, k in parts]
            near = [[coef(at, k, n) for n in range(3, COEFS)] for at, k in parts]
            partial = [[] for _ in parts]
            for g in range(count):
                at = e + g
                for t in range(steps):
                    here = [old[spot(at, k, t), :] for k in range(tiles)]
                    down = [pltpu.roll(value, 1, 0) for value in here]
                    up = [pltpu.roll(value, TILE - 1, 0) for value in here]
                    for k in range(wide):
                        n = g * wide + k
                        z_low, x_low, y_low, z_high, x_high, y_high = near[n]
                        below = jnp.where(row == 0, down[k - 1], down[k])
                        above = jnp.where(row == TILE - 1, up[(k + 1) % tiles], up[k])
                        total = self.source[spot(at, k, t), :] + z_low * old[spot(at - 1, k, t), :]
                        total = total + z_high * old[spot(at + 1, k, t), :]
                        total = total + (x_low * below + x_high * above)
                        total = total + (
                            y_low * pltpu.roll(here[k], 1, 1) + y_high * pltpu.roll(here[k], ny - 1, 1)
                        )
                        if t:
                            total = total + c[n] * partial[n][-1]
                        partial[n].append(total)
            for n, (at, k) in enumerate(parts):
                carry = c[n] * (coef(at, k, 2) * partial[n][-1])
                for t in range(steps):
                    value = partial[n][t] + carry
                    carry = c[n] * carry
                    if final:
                        self.last[rows_at((t * plan.nz + at - GHOST) * plan.main + k), :] = value
                    else:
                        new[spot(at, k, t), :] = value

        if total is not None:

            def several(i, _):
                layers(start + i * GROUP, GROUP)
                return 0

            lax.fori_loop(0, total // GROUP, several, 0)
            if total % GROUP:
                layers(start + total // GROUP * GROUP, total % GROUP)
        else:

            def one(e, _):
                layers(e, 1)
                return 0

            lax.fori_loop(start, stop, one, 0)


def first_pass(plan, work, ghost, start, count):
    def layer(z):
        work.first(z + GHOST, plan.main, [ghost[rows_at(t * plan.nz + z), :] for t in range(plan.steps)])

    def several(i, _):
        for n in range(4):
            layer(start + i * 4 + n)
        return 0

    lax.fori_loop(0, count // 4, several, 0)
    for n in range(count // 4 * 4, count):
        layer(start + n)


def ghost_pass(plan, place, work, z_in):
    steps, main, sides, deep = plan.steps, plan.main, plan.sides, GHOST - 1
    coefs, source, ping = work.coefs, work.source, work.buffers[0]
    empty = jnp.zeros((TILE, plan.ny), jnp.float32)

    def ghost_layers(at, upper, z_ref):
        for n in range(GHOST):
            e = at + n
            for k in range(plan.tiles):
                raw = steps * plan.z_tiles + (n * plan.tiles + k) * RAW

                def store(number, value, k=k, e=e):
                    coefs[rows_at((e * plan.tiles + k) * COEFS + number), :] = value

                write_coefs(plan, place.hi, None, k, [z_ref[rows_at(raw + m), :] for m in range(RAW)], store)
            for k in range(main):
                tile = n * main + k
                work.first(e, k, [z_ref[rows_at(t * plan.z_tiles + tile), :] for t in range(steps)], True)
            c_at = n if upper else n - (GHOST - deep)
            if 0 <= c_at < deep:
                tile = GHOST * main + c_at
                work.first(e, main, [z_ref[rows_at(t * plan.z_tiles + tile), :] for t in range(steps)])
            else:
                for t in range(steps):
                    ping[work.spot(e, main, t), :] = empty
                    source[work.spot(e, main, t), :] = empty

    for odd in (False, True):

        @pl.when(work.has_low & (place.zb_odd == odd))
        def _(odd=odd):
            ghost_layers(0, False, z_in[0 if odd else sides - 1])

        @pl.when(work.has_high & (place.zb_odd == odd))
        def _(odd=odd):
            ghost_layers(work.high_at, True, z_in[sides - 1 if odd else 0])


def no_ghosts(plan, work):
    empty = jnp.zeros((TILE, plan.ny), jnp.float32)
    for outside, e in ((work.has_low, work.low_at - 1), (work.has_high, work.high_at)):

        @pl.when(jnp.logical_not(outside))
        def _(e=e):
            for k in range(plan.tiles):
                for t in range(plan.steps):
                    for buffer in work.buffers:
                        buffer[work.spot(e, k, t), :] = empty


def write_piece(plan, place, last, outs, number):
    for out, (r, piece) in zip(outs, plan.back[number]):
        start = 0 if piece is None else place.piece(plan, piece)
        at = ((place.t ^ r) * plan.nz + start) * plan.rows
        out[...] = last[pl.ds(pl.multiple_of(at, TILE), out.shape[0]), :]


def all_sweeps(plan, place_ref, coefs_in, source_in, ping_in, ghost, *refs):
    place = Place(plan, place_ref)
    z_in, refs = refs[: plan.sides], refs[plan.sides :]
    outs, (coefs, source, ping, pong, last) = refs[:-5], refs[-5:]
    work = Sweeps(plan, place, coefs, source, ping, pong, last)
    first_pass(plan, work, ghost, 0, plan.nz)
    ghost_pass(plan, place, work, z_in)
    no_ghosts(plan, work)
    for number in range(1, SWEEPS):
        reach = SWEEPS - 1 - number
        start = work.low_at - jnp.where(work.has_low, reach, 0)
        stop = work.high_at + jnp.where(work.has_high, reach, 0)
        work.sweep(number, start, stop)
    write_piece(plan, place, last, outs, 0)


def far_sweeps(plan, place_ref, coefs, source_in, ping_in, *refs):
    place = Place(plan, place_ref)
    given, refs = refs[: plan.ghost_inputs], refs[plan.ghost_inputs :]
    outs, (source, ping, pong, last, ghost, z_send, planes) = refs[:-7], refs[-7:]
    gather_ghosts(plan, place_ref, source, *given, ghost, z_send, planes)
    work = Sweeps(plan, place, coefs, source, ping, pong, last)
    count = plan.pieces()[0]
    first_pass(plan, work, ghost, jnp.where(place.up, 0, plan.nz - count - GHOST), count + GHOST)
    no_ghosts(plan, work)
    for number in range(1, SWEEPS):
        total = count + SWEEPS - 1 - number
        start = jnp.where(place.up, work.low_at, work.high_at - total)
        work.sweep(number, start, start + total, total)
    write_piece(plan, place, last, outs, 0)


def near_sweeps(plan, place_ref, ghost, z_in, coefs_in, source_in, ping_in, pong_in, last_in, *refs):
    place = Place(plan, place_ref)
    outs, (coefs, source, ping, pong, last) = refs[:-5], refs[-5:]
    work = Sweeps(plan, place, coefs, source, ping, pong, last)
    first, count = plan.pieces()
    left = plan.nz - first - GHOST
    first_pass(plan, work, ghost, jnp.where(place.up, plan.nz - left, 0), left)
    ghost_pass(plan, place, work, [z_in])
    for number in range(1, SWEEPS):
        reach = SWEEPS - 1 - number
        start = jnp.where(place.up, work.low_at + first + reach, work.low_at - reach)
        work.sweep(number, start, start + count, count)
    write_piece(plan, place, last, outs, 1)


def run_sweeps(plan, call, coefs, source, ping, ghost_inputs):
    steps, ny = plan.steps, plan.ny
    grid = (plan.ext * plan.tiles * steps * TILE, ny)
    whole = (steps * plan.nz * plan.rows, ny)
    ghost = (steps * plan.nz * TILE, ny)
    z_send = ((steps * plan.z_tiles + plan.raw_tiles) * TILE, ny)
    planes = pltpu.VMEM((steps // 2 * plan.nz * TILE, ny), jnp.float32)
    shapes = [[(plan.layers(piece) * plan.rows, ny) for r, piece in blocks] for blocks in plan.back]

    def along_z(sends):
        return [lax.ppermute(send, FLAT, plan.z_pairs(first)) for first, send in enumerate(sends)]

    if len(shapes) == 1:
        ghost, *z_sends = call(
            gather_ghosts, [ghost] + [z_send] * plan.sides, (source, *ghost_inputs), scratch=[planes]
        )
        found = call(
            all_sweeps,
            shapes[0] + [coefs.shape, grid, grid],
            (coefs, source, ping, ghost, *along_z(z_sends)),
            scratch=[pltpu.VMEM(shape, jnp.float32) for shape in (grid, whole)],
            aliases={1 + n: len(shapes[0]) + n for n in range(3)},
            limit=24,
        )
        return [found[:-3]]
    *done, source, ping, pong, last, ghost, z_send = call(
        far_sweeps,
        shapes[0] + [grid] * 3 + [whole, ghost, z_send],
        (coefs, source, ping, *ghost_inputs),
        scratch=[planes],
        aliases={2 + n: len(shapes[0]) + n for n in range(2)},
        limit=24,
    )
    rest = call(
        near_sweeps,
        shapes[1] + [coefs.shape] + [grid] * 3 + [whole],
        (ghost, *along_z([z_send]), coefs, source, ping, pong, last),
        aliases={3 + n: len(shapes[1]) + n for n in range(5)},
        limit=24,
    )
    return [done, rest[:-5]]


def place_blocks(plan, place_ref, *refs):
    place = Place(plan, place_ref)
    blocks, (out, sems) = refs[:-2], refs[-2:]
    copies = []
    for n, (block, (r, piece)) in enumerate(zip(blocks, sum(plan.back, []))):
        source = place.t ^ r
        quarter, lo = source // plan.per_quarter, source % plan.per_quarter
        z = lo // 2 * plan.nz + (0 if piece is None else place.piece(plan, piece))
        x = pl.multiple_of(quarter * plan.rows, plan.rows)
        target = out.at[lo % 2, pl.ds(z, plan.layers(piece)), pl.ds(x, plan.rows), :]
        copies.append(pltpu.make_async_copy(block, target, sems.at[n]))
    for copy in copies:
        copy.start()
    for copy in copies:
        copy.wait()


def local(right_side, diffusivity, velocity):
    steps, cores = lax.axis_size("tm"), lax.axis_size("space")
    _, parts, half_z, nx, ny = right_side.shape
    plan = Plan(steps, cores, half_z, nx, ny)
    place = jnp.stack([lax.axis_index("tm"), lax.axis_index("space")]).astype(jnp.int32)
    size = plan.nz * plan.rows
    half_x = steps // 2 * plan.nz

    def call(body, outs, arrays, extra=None, **options):
        body = functools.partial(body, plan) if extra is None else functools.partial(body, plan, extra)
        return kernel_call(body, outs, (place, *arrays), **options)

    def turned(arrays, rounds, ties=(), known=()):
        found = list(known)
        for n, (array, r) in enumerate(zip(arrays, rounds), len(found)):
            for late, early in ties:
                if n == late:
                    array, found[early] = lax.optimization_barrier((array, found[early]))
            found.append(array if r == 0 else lax.ppermute(array, "tm", plan.pairs(r)))
        return found

    sends = call(
        pack_blocks,
        [(plan.nz * plan.stride(r), ny) for r in plan.rounds],
        (right_side.reshape(parts * half_z * nx, ny),),
        extra=plan.rounds,
    )
    blocks = turned(sends, plan.rounds)
    blocks = lax.optimization_barrier(blocks)
    x_even, x_odd = call(edge_rows, [(GHOST * half_x, ny)] * 2, blocks)
    even = lax.ppermute(x_even, "tm", plan.x_pairs(0))
    odd = lax.ppermute(x_odd, "tm", plan.x_pairs(1))
    diffusivity, velocity, *blocks = lax.optimization_barrier((diffusivity, velocity, *blocks))
    coefs, *raws = call(
        make_coefs,
        [(plan.ext * plan.tiles * COEFS * TILE, ny)] + [(plan.raw_tiles * TILE, ny)] * plan.sides,
        (diffusivity.reshape(half_z * nx, ny), velocity.reshape(3 * half_z * nx, ny)),
    )
    direct = [block for block, r in zip(blocks, plan.rounds) if plan.direct(r)]
    grid = (plan.ext * plan.tiles * steps * TILE, ny)
    source, ping = call(
        first_own, [grid, grid], (coefs, *blocks), scratch=[pltpu.VMEM((steps * size, ny), jnp.float32)]
    )
    solved = run_sweeps(plan, call, coefs, source, ping, (even, odd, *direct, *raws))
    back = []
    for found, blocks in zip(solved, plan.back):
        back = turned(found, [r for r, piece in blocks], plan.ties, back)
    back = [
        block.reshape(plan.layers(piece), plan.rows, ny) for block, (r, piece) in zip(back, sum(plan.back, []))
    ]
    out = call(
        place_blocks,
        (parts, half_z, nx, ny),
        back,
        scratch=[pltpu.SemaphoreType.DMA((len(back),))],
        out_space=pltpu.HBM,
    )
    return out[None]


def solution(mesh):
    placed = (
        P(("group", "tm"), None, "space", None, None),
        P("space", None, None),
        P(None, "space", None, None),
    )
    return jax.shard_map(
        local,
        mesh=mesh,
        in_specs=placed,
        out_specs=P(("group", "tm"), None, "space", None, None),
        check_vma=False,
    )
```

```python
import functools

import jax
import jax.numpy as jnp
from jax import lax
from jax.experimental import pallas as pl
from jax.experimental.pallas import tpu as pltpu
from jax.sharding import PartitionSpec as P

SWEEPS = 4
GHOST = SWEEPS - 1
QUARTERS = 4
TILE = 8
COEFS = 9
RAW = 4
GROUP = 6
EARLY = 6

alpha_circ = 0.1
inv_step = 2.0

FLAT = ("tm", "space")


class Plan:
    def __init__(self, steps, cores, half_z, nx, ny):
        self.steps, self.cores, self.half_z, self.nx, self.ny = steps, cores, half_z, nx, ny
        self.per_quarter = steps // QUARTERS
        self.in_half = self.per_quarter // 2
        self.z_parts = self.in_half * cores
        self.nz = half_z // self.in_half
        self.rows = nx // QUARTERS
        self.main = self.rows // TILE
        self.tiles = self.main + 1
        self.ext = self.nz + 2 * GHOST
        self.sides = 1 if self.z_parts == 2 else 2
        self.z_tiles = GHOST * self.main + GHOST - 1
        self.raw_tiles = GHOST * self.tiles * RAW
        self.ghost_inputs = 2 + steps // 2 + self.sides
        kinds = [(2, 0), (1, 0), (1, 1), (0, 1), (2, 1), (3, 0), (3, 1), (0, 0)]
        self.rounds = [a * self.per_quarter + m * 2 + c for m in range(self.in_half) for a, c in kinds]

        self.back, self.ties = self.return_order()

    def return_order(self):
        pieces = len(self.pieces())
        near = [r for r in self.rounds if self.direct(r)]
        far = [r for r in self.rounds if not self.direct(r)]
        if pieces == 1:
            return [[(r, None) for r in far + near]], ()
        far = far[2:] + far[:2]
        back = [[(r, 0) for r in far], [(r, 1) for r in far] + [(r, None) for r in near]]
        return back, [(2 * len(far) + n, len(far) - 1) for n in range(len(near) - 1)]

    def pieces(self):
        if self.sides == 1 and self.nz >= 4 * GHOST:
            return [self.nz // 2, self.nz // 2]
        return [self.nz]

    def layers(self, piece):
        return self.nz if piece is None else self.pieces()[piece]

    def direct(self, r):
        return r // self.per_quarter < 2

    def stride(self, r):
        return self.rows + TILE if self.direct(r) else self.rows

    def pairs(self, r):
        return [(i, i ^ r) for i in range(self.steps)]

    def x_pairs(self, first):
        result = []
        for hi in range(first, QUARTERS - 1, 2):
            for lo in range(self.per_quarter):
                one = hi * self.per_quarter + lo
                result += [(one, one + self.per_quarter), (one + self.per_quarter, one)]
        return result

    def z_pairs(self, first):
        def flat(hi, zb, part):
            return (hi * self.per_quarter + zb % self.in_half * 2 + part) * self.cores + zb // self.in_half

        result = []
        for zb in range(first, self.z_parts - 1, 2):
            for hi in range(QUARTERS):
                for part in range(2):
                    one, two = flat(hi, zb, part), flat(hi, zb + 1, part)
                    result += [(one, two), (two, one)]
        return result


class Place:
    def __init__(self, plan, ref):
        self.t, self.s = ref[0], ref[1]
        self.hi, self.lo = self.t // plan.per_quarter, self.t % plan.per_quarter
        self.zm, self.part = self.lo // 2, self.lo % 2
        self.zb = self.s * plan.in_half + self.zm
        self.hi_odd, self.zb_odd = self.hi % 2 == 1, self.zb % 2 == 1
        self.up = self.zb == 0

    def piece(self, plan, number):
        sizes = plan.pieces()
        before = sum(sizes[:number])
        if len(sizes) == 1:
            return 0
        return jnp.where(self.up, before, plan.nz - before - sizes[number])


def kernel_call(body, outs, args, scratch=(), spaces=None, out_space=pltpu.VMEM, limit=16, aliases=None):
    spaces = [pltpu.SMEM] + (spaces or [pltpu.VMEM] * (len(args) - 1))
    single = isinstance(outs, tuple)
    shapes = [outs] if single else list(outs)
    result = pl.pallas_call(
        body,
        out_shape=[jax.ShapeDtypeStruct(s, jnp.float32) for s in shapes],
        in_specs=[pl.BlockSpec(memory_space=space) for space in spaces],
        out_specs=[pl.BlockSpec(memory_space=out_space)] * len(shapes),
        scratch_shapes=list(scratch),
        input_output_aliases=aliases or {},
        compiler_params=pltpu.CompilerParams(vmem_limit_bytes=limit << 20),
    )(*args)
    return result[0] if single else result


def rows_at(index, count=1):
    return pl.ds(pl.multiple_of(index * TILE, TILE), count * TILE)


def sublane(plan):
    return lax.broadcasted_iota(jnp.int32, (TILE, plan.ny), 0)


def lane(plan):
    return lax.broadcasted_iota(jnp.int32, (TILE, plan.ny), 1)


def near_tiles(plan, hi):
    per = plan.nx // TILE
    own = [hi * plan.main + k for k in range(plan.main)]
    return own, jnp.minimum(own[-1] + 1, per - 1), jnp.maximum(own[0] - 1, 0)


def write_coefs(plan, hi, inside, k, values, store):
    row, col = sublane(plan), lane(plan)
    d, vz, vx, vy = values
    if k < plan.main:
        x = row + k * TILE
    else:
        x = jnp.where(row < GHOST, row + plan.rows, row - TILE)
    x = x + hi * plan.rows
    keep = (x >= 0) & (x < plan.nx)
    if k == plan.main:
        keep = keep & ((row < GHOST) | (row >= TILE - GHOST))
    if inside is not None:
        keep = keep & inside
    total = inv_step + 6.0 * d + (jnp.abs(vz) + jnp.abs(vx) + jnp.abs(vy))
    w = jnp.where(keep, 1.0 / total, 0.0)
    c = inv_step * w
    power = c
    for _ in range(plan.steps.bit_length() - 1):
        power = power * power
    wrap = alpha_circ / (1.0 - alpha_circ * power)
    low = [w * (d + jnp.maximum(v, 0.0)) for v in (vz, vx, vy)]
    high = [w * (d + jnp.maximum(-v, 0.0)) for v in (vz, vx, vy)]
    low[2] = jnp.where(col == 0, 0.0, low[2])
    high[2] = jnp.where(col == plan.ny - 1, 0.0, high[2])
    for n, value in enumerate([w, c, wrap] + low + high):
        store(n, value)


def make_coefs(plan, place_ref, d_ref, v_ref, out_ref, *raw_refs):
    place = Place(plan, place_ref)
    per = plan.nx // TILE
    row = sublane(plan)
    own, over, under = near_tiles(plan, place.hi)

    def read(z):
        z = place.zm * plan.nz + z
        found = []
        for n in range(RAW):
            ref, base = (d_ref, z * per) if n == 0 else (v_ref, ((n - 1) * plan.half_z + z) * per)
            edge = jnp.where(row < TILE // 2, ref[rows_at(base + over), :], ref[rows_at(base + under), :])
            found.append([ref[rows_at(base + at), :] for at in own] + [edge])
        return [[tiles[k] for tiles in found] for k in range(plan.tiles)]

    def layer(z, _):
        for k, values in enumerate(read(z)):

            def store(n, value, k=k):
                out_ref[rows_at(((z + GHOST) * plan.tiles + k) * COEFS + n), :] = value

            write_coefs(plan, place.hi, None, k, values, store)
        return 0

    lax.fori_loop(0, plan.nz, layer, 0)
    for side, raw in enumerate(raw_refs):
        up = jnp.logical_not(place.zb_odd) if side == 0 else place.zb_odd
        for n in range(GHOST):
            for k, values in enumerate(read(jnp.where(up, plan.nz - GHOST + n, n))):
                for at, value in enumerate(values):
                    raw[rows_at((n * plan.tiles + k) * RAW + at), :] = value


def pack_blocks(plan, rounds, place_ref, right, *outs):
    place = Place(plan, place_ref)
    per = plan.nx // TILE
    row = sublane(plan)
    for out, r in zip(outs, rounds):
        target = place.t ^ r
        quarter, lo = target // plan.per_quarter, target % plan.per_quarter
        first = lo % 2 * plan.half_z + lo // 2 * plan.nz
        own, over, under = near_tiles(plan, quarter)
        tiles = plan.stride(r) // TILE
        for z in range(plan.nz):
            base = (first + z) * per
            for k, at in enumerate(own):
                out[rows_at(z * tiles + k), :] = right[rows_at(base + at), :]
            if plan.direct(r):
                edge = jnp.where(row < TILE // 2, right[rows_at(base + over), :], right[rows_at(base + under), :])
                out[rows_at(z * tiles + plan.main), :] = edge


def edge_rows(plan, place_ref, *refs):
    place = Place(plan, place_ref)
    blocks, (x_even, x_odd) = refs[: plan.steps], refs[plan.steps :]
    half = plan.steps // 2
    for block, r in zip(blocks, plan.rounds):
        step = (place.t ^ r) % half
        stride = plan.stride(r)
        for n in range(GHOST):
            low = block[pl.ds(n, plan.nz, stride=stride), :]
            high = block[pl.ds(plan.rows - GHOST + n, plan.nz, stride=stride), :]
            at = pl.ds((n * half + step) * plan.nz, plan.nz)
            if plan.direct(r):
                x_odd[at, :] = jnp.where(place.hi_odd, high, low)
            else:
                x_even[at, :] = jnp.where(place.hi_odd, low, high)


def first_own(plan, place_ref, coefs, *refs):
    place = Place(plan, place_ref)
    blocks, (source, ping, field) = refs[: plan.steps], refs[plan.steps :]
    size = plan.nz * plan.rows
    for block, r in zip(blocks, plan.rounds):
        at = (place.t ^ r) * size
        for z in range(plan.nz):
            to = pl.ds(pl.multiple_of(at + z * plan.rows, TILE), plan.rows)
            field[to, :] = block[pl.ds(z * plan.stride(r), plan.rows), :]
    work = Sweeps(plan, place, coefs, source, ping, None, None)

    def several(i, _):
        for n in range(4):
            z = i * 4 + n
            for k in range(plan.main):
                tiles = [field[rows_at((t * plan.nz + z) * plan.main + k), :] for t in range(plan.steps)]
                work.first(z + GHOST, k, tiles)
        return 0

    lax.fori_loop(0, plan.nz // 4, several, 0)


def gather_ghosts(plan, place_ref, source, even_ref, odd_ref, *refs):
    place = Place(plan, place_ref)
    direct = [r for r in plan.rounds if plan.direct(r)]
    blocks, refs = refs[: len(direct)], refs[len(direct) :]
    raws, refs = refs[: plan.sides], refs[plan.sides :]
    ghost, z_sends, planes = refs[0], refs[1:-1], refs[-1]
    half = plan.steps // 2
    count = half * plan.nz
    for block, r in zip(blocks, direct):
        at = (place.t ^ r) * plan.nz
        for z in range(plan.nz):
            ghost[rows_at(at + z), :] = block[pl.ds(z * plan.stride(r) + plan.rows, TILE), :]
    for n in range(GHOST):
        even, odd = even_ref[pl.ds(n * count, count), :], odd_ref[pl.ds(n * count, count), :]
        planes[pl.ds(n * count, count), :] = jnp.where(place.hi_odd, odd, even)
        planes[pl.ds((TILE - GHOST + n) * count, count), :] = jnp.where(place.hi_odd, even, odd)
    for n in range(GHOST, TILE - GHOST):
        planes[pl.ds(n * count, count), :] = jnp.zeros((count, plan.ny), jnp.float32)
    first = (1 - place.hi // 2) * count
    for n in range(count):
        ghost[rows_at(first + n), :] = planes[pl.ds(n, TILE, stride=count), :]
    deep, tiles = GHOST - 1, plan.z_tiles
    for side, (raw, z_send) in enumerate(zip(raws, z_sends)):
        up = jnp.logical_not(place.zb_odd) if side == 0 else place.zb_odd
        for t in range(plan.steps):
            for n in range(GHOST):
                e = GHOST + jnp.where(up, plan.nz - GHOST + n, n)
                for k in range(plan.main):
                    to = rows_at(t * tiles + n * plan.main + k)
                    z_send[to, :] = source[rows_at((e * plan.tiles + k) * plan.steps + t), :]
            for n in range(deep):
                z = t * plan.nz + jnp.where(up, plan.nz - deep + n, n)
                z_send[rows_at(t * tiles + GHOST * plan.main + n), :] = ghost[rows_at(z), :]
        z_send[rows_at(plan.steps * tiles, plan.raw_tiles), :] = raw[...]


class Sweeps:
    def __init__(self, plan, place, coefs, source, ping, pong, last):
        self.plan, self.coefs = plan, coefs
        self.source, self.buffers, self.last = source, (ping, pong), last
        self.has_low, self.has_high = place.zb > 0, place.zb < plan.z_parts - 1
        self.low_at, self.high_at = GHOST, GHOST + plan.nz

    def spot(self, e, k, t):
        return rows_at((e * self.plan.tiles + k) * self.plan.steps + t)

    def coef(self, e, k, n):
        return self.coefs[rows_at((e * self.plan.tiles + k) * COEFS + n), :]

    def first(self, e, k, values, scaled=False):
        w, c, wrap = (self.coef(e, k, n) for n in range(3))
        partial = []
        for t, value in enumerate(values):
            value = value if scaled else w * value
            self.source[self.spot(e, k, t), :] = value
            if t:
                value = value + c * partial[-1]
            partial.append(value)
        carry = c * (wrap * partial[-1])
        for t, value in enumerate(partial):
            self.buffers[0][self.spot(e, k, t), :] = value + carry
            carry = c * carry

    def sweep(self, number, start, stop, total=None):
        plan, steps, tiles, ny = self.plan, self.plan.steps, self.plan.tiles, self.plan.ny
        old, new = self.buffers[(number - 1) % 2], self.buffers[number % 2]
        final = number == SWEEPS - 1
        wide = plan.main if final else tiles
        row = sublane(plan)
        spot, coef = self.spot, self.coef

        def layers(e, count):
            parts = [(e + g, k) for g in range(count) for k in range(wide)]
            c = [coef(at, k, 1) for at, k in parts]
            near = [[coef(at, k, n) for n in range(3, COEFS)] for at, k in parts]
            partial = [[] for _ in parts]
            for g in range(count):
                at = e + g
                for t in range(steps):
                    here = [old[spot(at, k, t), :] for k in range(tiles)]
                    down = [pltpu.roll(value, 1, 0) for value in here]
                    up = [pltpu.roll(value, TILE - 1, 0) for value in here]
                    for k in range(wide):
                        n = g * wide + k
                        z_low, x_low, y_low, z_high, x_high, y_high = near[n]
                        below = jnp.where(row == 0, down[k - 1], down[k])
                        above = jnp.where(row == TILE - 1, up[(k + 1) % tiles], up[k])
                        total = self.source[spot(at, k, t), :] + z_low * old[spot(at - 1, k, t), :]
                        total = total + z_high * old[spot(at + 1, k, t), :]
                        total = total + (x_low * below + x_high * above)
                        total = total + (
                            y_low * pltpu.roll(here[k], 1, 1) + y_high * pltpu.roll(here[k], ny - 1, 1)
                        )
                        if t:
                            total = total + c[n] * partial[n][-1]
                        partial[n].append(total)
            for n, (at, k) in enumerate(parts):
                carry = c[n] * (coef(at, k, 2) * partial[n][-1])
                for t in range(steps):
                    value = partial[n][t] + carry
                    carry = c[n] * carry
                    if final:
                        self.last[rows_at((t * plan.nz + at - GHOST) * plan.main + k), :] = value
                    else:
                        new[spot(at, k, t), :] = value

        if total is not None:

            def several(i, _):
                layers(start + i * GROUP, GROUP)
                return 0

            lax.fori_loop(0, total // GROUP, several, 0)
            if total % GROUP:
                layers(start + total // GROUP * GROUP, total % GROUP)
        else:

            def one(e, _):
                layers(e, 1)
                return 0

            lax.fori_loop(start, stop, one, 0)


def first_pass(plan, work, ghost, start, count):
    def layer(z):
        work.first(z + GHOST, plan.main, [ghost[rows_at(t * plan.nz + z), :] for t in range(plan.steps)])

    def several(i, _):
        for n in range(4):
            layer(start + i * 4 + n)
        return 0

    lax.fori_loop(0, count // 4, several, 0)
    for n in range(count // 4 * 4, count):
        layer(start + n)


def ghost_pass(plan, place, work, z_in):
    steps, main, sides, deep = plan.steps, plan.main, plan.sides, GHOST - 1
    coefs, source, ping = work.coefs, work.source, work.buffers[0]
    empty = jnp.zeros((TILE, plan.ny), jnp.float32)

    def ghost_layers(at, upper, z_ref):
        for n in range(GHOST):
            e = at + n
            for k in range(plan.tiles):
                raw = steps * plan.z_tiles + (n * plan.tiles + k) * RAW

                def store(number, value, k=k, e=e):
                    coefs[rows_at((e * plan.tiles + k) * COEFS + number), :] = value

                write_coefs(plan, place.hi, None, k, [z_ref[rows_at(raw + m), :] for m in range(RAW)], store)
            for k in range(main):
                tile = n * main + k
                work.first(e, k, [z_ref[rows_at(t * plan.z_tiles + tile), :] for t in range(steps)], True)
            c_at = n if upper else n - (GHOST - deep)
            if 0 <= c_at < deep:
                tile = GHOST * main + c_at
                work.first(e, main, [z_ref[rows_at(t * plan.z_tiles + tile), :] for t in range(steps)])
            else:
                for t in range(steps):
                    ping[work.spot(e, main, t), :] = empty
                    source[work.spot(e, main, t), :] = empty

    for odd in (False, True):

        @pl.when(work.has_low & (place.zb_odd == odd))
        def _(odd=odd):
            ghost_layers(0, False, z_in[0 if odd else sides - 1])

        @pl.when(work.has_high & (place.zb_odd == odd))
        def _(odd=odd):
            ghost_layers(work.high_at, True, z_in[sides - 1 if odd else 0])


def no_ghosts(plan, work):
    empty = jnp.zeros((TILE, plan.ny), jnp.float32)
    for outside, e in ((work.has_low, work.low_at - 1), (work.has_high, work.high_at)):

        @pl.when(jnp.logical_not(outside))
        def _(e=e):
            for k in range(plan.tiles):
                for t in range(plan.steps):
                    for buffer in work.buffers:
                        buffer[work.spot(e, k, t), :] = empty


def write_piece(plan, place, last, outs, number):
    for out, (r, piece) in zip(outs, plan.back[number]):
        start = 0 if piece is None else place.piece(plan, piece)
        at = ((place.t ^ r) * plan.nz + start) * plan.rows
        out[...] = last[pl.ds(pl.multiple_of(at, TILE), out.shape[0]), :]


def all_sweeps(plan, place_ref, coefs_in, source_in, ping_in, ghost, *refs):
    place = Place(plan, place_ref)
    z_in, refs = refs[: plan.sides], refs[plan.sides :]
    outs, (coefs, source, ping, pong, last) = refs[:-5], refs[-5:]
    work = Sweeps(plan, place, coefs, source, ping, pong, last)
    first_pass(plan, work, ghost, 0, plan.nz)
    ghost_pass(plan, place, work, z_in)
    no_ghosts(plan, work)
    for number in range(1, SWEEPS):
        reach = SWEEPS - 1 - number
        start = work.low_at - jnp.where(work.has_low, reach, 0)
        stop = work.high_at + jnp.where(work.has_high, reach, 0)
        work.sweep(number, start, stop)
    write_piece(plan, place, last, outs, 0)


def far_sweeps(plan, place_ref, coefs, source_in, ping_in, *refs):
    place = Place(plan, place_ref)
    given, refs = refs[: plan.ghost_inputs], refs[plan.ghost_inputs :]
    outs, (source, ping, pong, last, ghost, z_send, planes) = refs[:-7], refs[-7:]
    gather_ghosts(plan, place_ref, source, *given, ghost, z_send, planes)
    work = Sweeps(plan, place, coefs, source, ping, pong, last)
    count = plan.pieces()[0]
    first_pass(plan, work, ghost, jnp.where(place.up, 0, plan.nz - count - GHOST), count + GHOST)
    no_ghosts(plan, work)
    for number in range(1, SWEEPS):
        total = count + SWEEPS - 1 - number
        start = jnp.where(place.up, work.low_at, work.high_at - total)
        work.sweep(number, start, start + total, total)
    write_piece(plan, place, last, outs, 0)


def near_sweeps(plan, place_ref, ghost, z_in, coefs_in, source_in, ping_in, pong_in, last_in, *refs):
    place = Place(plan, place_ref)
    outs, (coefs, source, ping, pong, last) = refs[:-5], refs[-5:]
    work = Sweeps(plan, place, coefs, source, ping, pong, last)
    first, count = plan.pieces()
    left = plan.nz - first - GHOST
    first_pass(plan, work, ghost, jnp.where(place.up, plan.nz - left, 0), left)
    ghost_pass(plan, place, work, [z_in])
    for number in range(1, SWEEPS):
        reach = SWEEPS - 1 - number
        start = jnp.where(place.up, work.low_at + first + reach, work.low_at - reach)
        work.sweep(number, start, start + count, count)
    write_piece(plan, place, last, outs, 1)


def run_sweeps(plan, call, coefs, source, ping, ghost_inputs):
    steps, ny = plan.steps, plan.ny
    grid = (plan.ext * plan.tiles * steps * TILE, ny)
    whole = (steps * plan.nz * plan.rows, ny)
    ghost = (steps * plan.nz * TILE, ny)
    z_send = ((steps * plan.z_tiles + plan.raw_tiles) * TILE, ny)
    planes = pltpu.VMEM((steps // 2 * plan.nz * TILE, ny), jnp.float32)
    shapes = [[(plan.layers(piece) * plan.rows, ny) for r, piece in blocks] for blocks in plan.back]

    def along_z(sends):
        return [lax.ppermute(send, FLAT, plan.z_pairs(first)) for first, send in enumerate(sends)]

    if len(shapes) == 1:
        ghost, *z_sends = call(
            gather_ghosts, [ghost] + [z_send] * plan.sides, (source, *ghost_inputs), scratch=[planes]
        )
        found = call(
            all_sweeps,
            shapes[0] + [coefs.shape, grid, grid],
            (coefs, source, ping, ghost, *along_z(z_sends)),
            scratch=[pltpu.VMEM(shape, jnp.float32) for shape in (grid, whole)],
            aliases={1 + n: len(shapes[0]) + n for n in range(3)},
            limit=24,
        )
        return [found[:-3]]
    *done, source, ping, pong, last, ghost, z_send = call(
        far_sweeps,
        shapes[0] + [grid] * 3 + [whole, ghost, z_send],
        (coefs, source, ping, *ghost_inputs),
        scratch=[planes],
        aliases={2 + n: len(shapes[0]) + n for n in range(2)},
        limit=24,
    )
    rest = call(
        near_sweeps,
        shapes[1] + [coefs.shape] + [grid] * 3 + [whole],
        (ghost, *along_z([z_send]), coefs, source, ping, pong, last),
        aliases={3 + n: len(shapes[1]) + n for n in range(5)},
        limit=24,
    )
    return [done, rest[:-5]]


def place_blocks(plan, listed, place_ref, *refs):
    place = Place(plan, place_ref)
    blocks, (out, sems) = refs[: len(listed)], refs[-2:]
    copies = []
    for n, (block, (r, piece)) in enumerate(zip(blocks, listed)):
        source = place.t ^ r
        quarter, lo = source // plan.per_quarter, source % plan.per_quarter
        z = lo // 2 * plan.nz + (0 if piece is None else place.piece(plan, piece))
        x = pl.multiple_of(quarter * plan.rows, plan.rows)
        target = out.at[lo % 2, pl.ds(z, plan.layers(piece)), pl.ds(x, plan.rows), :]
        copies.append(pltpu.make_async_copy(block, target, sems.at[n]))
    for copy in copies:
        copy.start()
    for copy in copies:
        copy.wait()


def local(right_side, diffusivity, velocity):
    steps, cores = lax.axis_size("tm"), lax.axis_size("space")
    _, parts, half_z, nx, ny = right_side.shape
    plan = Plan(steps, cores, half_z, nx, ny)
    place = jnp.stack([lax.axis_index("tm"), lax.axis_index("space")]).astype(jnp.int32)
    size = plan.nz * plan.rows
    half_x = steps // 2 * plan.nz

    def call(body, outs, arrays, extra=None, **options):
        body = functools.partial(body, plan) if extra is None else functools.partial(body, plan, extra)
        return kernel_call(body, outs, (place, *arrays), **options)

    def turned(arrays, rounds, ties=(), known=()):
        found = list(known)
        for n, (array, r) in enumerate(zip(arrays, rounds), len(found)):
            for late, early in ties:
                if n == late:
                    array, found[early] = lax.optimization_barrier((array, found[early]))
            found.append(array if r == 0 else lax.ppermute(array, "tm", plan.pairs(r)))
        return found

    sends = call(
        pack_blocks,
        [(plan.nz * plan.stride(r), ny) for r in plan.rounds],
        (right_side.reshape(parts * half_z * nx, ny),),
        extra=plan.rounds,
    )
    blocks = turned(sends, plan.rounds)
    blocks = lax.optimization_barrier(blocks)
    x_even, x_odd = call(edge_rows, [(GHOST * half_x, ny)] * 2, blocks)
    even = lax.ppermute(x_even, "tm", plan.x_pairs(0))
    odd = lax.ppermute(x_odd, "tm", plan.x_pairs(1))
    diffusivity, velocity, *blocks = lax.optimization_barrier((diffusivity, velocity, *blocks))
    coefs, *raws = call(
        make_coefs,
        [(plan.ext * plan.tiles * COEFS * TILE, ny)] + [(plan.raw_tiles * TILE, ny)] * plan.sides,
        (diffusivity.reshape(half_z * nx, ny), velocity.reshape(3 * half_z * nx, ny)),
    )
    direct = [block for block, r in zip(blocks, plan.rounds) if plan.direct(r)]
    grid = (plan.ext * plan.tiles * steps * TILE, ny)
    source, ping = call(
        first_own, [grid, grid], (coefs, *blocks), scratch=[pltpu.VMEM((steps * size, ny), jnp.float32)]
    )
    solved = run_sweeps(plan, call, coefs, source, ping, (even, odd, *direct, *raws))
    back = []
    for found, blocks in zip(solved, plan.back):
        back = turned(found, [r for r, piece in blocks], plan.ties, back)
    back = [
        block.reshape(plan.layers(piece), plan.rows, ny) for block, (r, piece) in zip(back, sum(plan.back, []))
    ]
    listed = sum(plan.back, [])
    cut = EARLY if len(plan.back) == 2 else 0
    begun = []
    for chosen in (range(cut), range(cut, len(back))):
        if len(chosen):
            out = call(
                place_blocks,
                (parts, half_z, nx, ny),
                [back[n] for n in chosen] + begun,
                extra=[listed[n] for n in chosen],
                spaces=[pltpu.VMEM] * len(chosen) + [pltpu.HBM] * len(begun),
                scratch=[pltpu.SemaphoreType.DMA((len(chosen),))],
                out_space=pltpu.HBM,
                aliases={1 + len(chosen): 0} if begun else None,
            )
            begun = [out]
    return out[None]


def solution(mesh):
    placed = (
        P(("group", "tm"), None, "space", None, None),
        P("space", None, None),
        P(None, "space", None, None),
    )
    return jax.shard_map(
        local,
        mesh=mesh,
        in_specs=placed,
        out_specs=P(("group", "tm"), None, "space", None, None),
        check_vma=False,
    )
```

```python
import functools

import jax
import jax.numpy as jnp
from jax import lax
from jax.experimental import pallas as pl
from jax.experimental.pallas import tpu as pltpu
from jax.sharding import PartitionSpec as P

SWEEPS = 4
GHOST = SWEEPS - 1
QUARTERS = 4
TILE = 8
COEFS = 9
RAW = 4
GROUP = 10
EARLY = 6

alpha_circ = 0.1
inv_step = 2.0

FLAT = ("tm", "space")


class Plan:
    def __init__(self, steps, cores, half_z, nx, ny):
        self.steps, self.cores, self.half_z, self.nx, self.ny = steps, cores, half_z, nx, ny
        self.per_quarter = steps // QUARTERS
        self.in_half = self.per_quarter // 2
        self.z_parts = self.in_half * cores
        self.nz = half_z // self.in_half
        self.rows = nx // QUARTERS
        self.main = self.rows // TILE
        self.tiles = self.main + 1
        self.ext = self.nz + 2 * GHOST
        self.sides = 1 if self.z_parts == 2 else 2
        self.z_tiles = GHOST * self.main + GHOST - 1
        self.raw_tiles = GHOST * self.tiles * RAW
        self.ghost_inputs = 2 + steps // 2 + self.sides
        kinds = [(2, 0), (1, 0), (1, 1), (0, 1), (2, 1), (3, 0), (3, 1), (0, 0)]
        self.rounds = [a * self.per_quarter + m * 2 + c for m in range(self.in_half) for a, c in kinds]

        self.back, self.ties = self.return_order()

    def return_order(self):
        pieces = len(self.pieces())
        near = [r for r in self.rounds if self.direct(r)]
        far = [r for r in self.rounds if not self.direct(r)]
        if pieces == 1:
            return [[(r, None) for r in far + near]], ()
        far = far[2:] + far[:2]
        back = [[(r, 0) for r in far], [(r, 1) for r in far] + [(r, None) for r in near]]
        return back, [(2 * len(far) + n, len(far) - 1) for n in range(len(near) - 1)]

    def pieces(self):
        if self.sides == 1 and self.nz >= 4 * GHOST:
            return [self.nz // 2, self.nz // 2]
        return [self.nz]

    def layers(self, piece):
        return self.nz if piece is None else self.pieces()[piece]

    def direct(self, r):
        return r // self.per_quarter < 2

    def stride(self, r):
        return self.rows + TILE if self.direct(r) else self.rows

    def pairs(self, r):
        return [(i, i ^ r) for i in range(self.steps)]

    def x_pairs(self, first):
        result = []
        for hi in range(first, QUARTERS - 1, 2):
            for lo in range(self.per_quarter):
                one = hi * self.per_quarter + lo
                result += [(one, one + self.per_quarter), (one + self.per_quarter, one)]
        return result

    def z_pairs(self, first):
        def flat(hi, zb, part):
            return (hi * self.per_quarter + zb % self.in_half * 2 + part) * self.cores + zb // self.in_half

        result = []
        for zb in range(first, self.z_parts - 1, 2):
            for hi in range(QUARTERS):
                for part in range(2):
                    one, two = flat(hi, zb, part), flat(hi, zb + 1, part)
                    result += [(one, two), (two, one)]
        return result


class Place:
    def __init__(self, plan, ref):
        self.t, self.s = ref[0], ref[1]
        self.hi, self.lo = self.t // plan.per_quarter, self.t % plan.per_quarter
        self.zm, self.part = self.lo // 2, self.lo % 2
        self.zb = self.s * plan.in_half + self.zm
        self.hi_odd, self.zb_odd = self.hi % 2 == 1, self.zb % 2 == 1
        self.up = self.zb == 0

    def piece(self, plan, number):
        sizes = plan.pieces()
        before = sum(sizes[:number])
        if len(sizes) == 1:
            return 0
        return jnp.where(self.up, before, plan.nz - before - sizes[number])


def kernel_call(body, outs, args, scratch=(), spaces=None, out_space=pltpu.VMEM, limit=16, aliases=None):
    spaces = [pltpu.SMEM] + (spaces or [pltpu.VMEM] * (len(args) - 1))
    single = isinstance(outs, tuple)
    shapes = [outs] if single else list(outs)
    result = pl.pallas_call(
        body,
        out_shape=[jax.ShapeDtypeStruct(s, jnp.float32) for s in shapes],
        in_specs=[pl.BlockSpec(memory_space=space) for space in spaces],
        out_specs=[pl.BlockSpec(memory_space=out_space)] * len(shapes),
        scratch_shapes=list(scratch),
        input_output_aliases=aliases or {},
        compiler_params=pltpu.CompilerParams(vmem_limit_bytes=limit << 20),
    )(*args)
    return result[0] if single else result


def rows_at(index, count=1):
    return pl.ds(pl.multiple_of(index * TILE, TILE), count * TILE)


def sublane(plan):
    return lax.broadcasted_iota(jnp.int32, (TILE, plan.ny), 0)


def lane(plan):
    return lax.broadcasted_iota(jnp.int32, (TILE, plan.ny), 1)


def near_tiles(plan, hi):
    per = plan.nx // TILE
    own = [hi * plan.main + k for k in range(plan.main)]
    return own, jnp.minimum(own[-1] + 1, per - 1), jnp.maximum(own[0] - 1, 0)


def write_coefs(plan, hi, inside, k, values, store):
    row, col = sublane(plan), lane(plan)
    d, vz, vx, vy = values
    if k < plan.main:
        x = row + k * TILE
    else:
        x = jnp.where(row < GHOST, row + plan.rows, row - TILE)
    x = x + hi * plan.rows
    keep = (x >= 0) & (x < plan.nx)
    if k == plan.main:
        keep = keep & ((row < GHOST) | (row >= TILE - GHOST))
    if inside is not None:
        keep = keep & inside
    total = inv_step + 6.0 * d + (jnp.abs(vz) + jnp.abs(vx) + jnp.abs(vy))
    w = jnp.where(keep, 1.0 / total, 0.0)
    c = inv_step * w
    power = c
    for _ in range(plan.steps.bit_length() - 1):
        power = power * power
    wrap = alpha_circ / (1.0 - alpha_circ * power)
    low = [w * (d + jnp.maximum(v, 0.0)) for v in (vz, vx, vy)]
    high = [w * (d + jnp.maximum(-v, 0.0)) for v in (vz, vx, vy)]
    low[2] = jnp.where(col == 0, 0.0, low[2])
    high[2] = jnp.where(col == plan.ny - 1, 0.0, high[2])
    for n, value in enumerate([w, c, wrap] + low + high):
        store(n, value)


def make_coefs(plan, place_ref, d_ref, v_ref, out_ref, *raw_refs):
    place = Place(plan, place_ref)
    per = plan.nx // TILE
    row = sublane(plan)
    own, over, under = near_tiles(plan, place.hi)

    def read(z):
        z = place.zm * plan.nz + z
        found = []
        for n in range(RAW):
            ref, base = (d_ref, z * per) if n == 0 else (v_ref, ((n - 1) * plan.half_z + z) * per)
            edge = jnp.where(row < TILE // 2, ref[rows_at(base + over), :], ref[rows_at(base + under), :])
            found.append([ref[rows_at(base + at), :] for at in own] + [edge])
        return [[tiles[k] for tiles in found] for k in range(plan.tiles)]

    def layer(z, _):
        for k, values in enumerate(read(z)):

            def store(n, value, k=k):
                out_ref[rows_at(((z + GHOST) * plan.tiles + k) * COEFS + n), :] = value

            write_coefs(plan, place.hi, None, k, values, store)
        return 0

    lax.fori_loop(0, plan.nz, layer, 0)
    for side, raw in enumerate(raw_refs):
        up = jnp.logical_not(place.zb_odd) if side == 0 else place.zb_odd
        for n in range(GHOST):
            for k, values in enumerate(read(jnp.where(up, plan.nz - GHOST + n, n))):
                for at, value in enumerate(values):
                    raw[rows_at((n * plan.tiles + k) * RAW + at), :] = value


def pack_blocks(plan, rounds, place_ref, right, *outs):
    place = Place(plan, place_ref)
    per = plan.nx // TILE
    row = sublane(plan)
    for out, r in zip(outs, rounds):
        target = place.t ^ r
        quarter, lo = target // plan.per_quarter, target % plan.per_quarter
        first = lo % 2 * plan.half_z + lo // 2 * plan.nz
        own, over, under = near_tiles(plan, quarter)
        tiles = plan.stride(r) // TILE
        for z in range(plan.nz):
            base = (first + z) * per
            for k, at in enumerate(own):
                out[rows_at(z * tiles + k), :] = right[rows_at(base + at), :]
            if plan.direct(r):
                edge = jnp.where(row < TILE // 2, right[rows_at(base + over), :], right[rows_at(base + under), :])
                out[rows_at(z * tiles + plan.main), :] = edge


def edge_rows(plan, place_ref, *refs):
    place = Place(plan, place_ref)
    blocks, (x_even, x_odd) = refs[: plan.steps], refs[plan.steps :]
    half = plan.steps // 2
    for block, r in zip(blocks, plan.rounds):
        step = (place.t ^ r) % half
        stride = plan.stride(r)
        for n in range(GHOST):
            low = block[pl.ds(n, plan.nz, stride=stride), :]
            high = block[pl.ds(plan.rows - GHOST + n, plan.nz, stride=stride), :]
            at = pl.ds((n * half + step) * plan.nz, plan.nz)
            if plan.direct(r):
                x_odd[at, :] = jnp.where(place.hi_odd, high, low)
            else:
                x_even[at, :] = jnp.where(place.hi_odd, low, high)


def first_own(plan, place_ref, coefs, *refs):
    place = Place(plan, place_ref)
    blocks, (source, ping, field) = refs[: plan.steps], refs[plan.steps :]
    size = plan.nz * plan.rows
    for block, r in zip(blocks, plan.rounds):
        at = (place.t ^ r) * size
        for z in range(plan.nz):
            to = pl.ds(pl.multiple_of(at + z * plan.rows, TILE), plan.rows)
            field[to, :] = block[pl.ds(z * plan.stride(r), plan.rows), :]
    work = Sweeps(plan, place, coefs, source, ping, None, None)

    def several(i, _):
        for n in range(4):
            z = i * 4 + n
            for k in range(plan.main):
                tiles = [field[rows_at((t * plan.nz + z) * plan.main + k), :] for t in range(plan.steps)]
                work.first(z + GHOST, k, tiles)
        return 0

    lax.fori_loop(0, plan.nz // 4, several, 0)


def gather_ghosts(plan, place_ref, source, even_ref, odd_ref, *refs):
    place = Place(plan, place_ref)
    direct = [r for r in plan.rounds if plan.direct(r)]
    blocks, refs = refs[: len(direct)], refs[len(direct) :]
    raws, refs = refs[: plan.sides], refs[plan.sides :]
    ghost, z_sends, planes = refs[0], refs[1:-1], refs[-1]
    half = plan.steps // 2
    count = half * plan.nz
    for block, r in zip(blocks, direct):
        at = (place.t ^ r) * plan.nz
        for z in range(plan.nz):
            ghost[rows_at(at + z), :] = block[pl.ds(z * plan.stride(r) + plan.rows, TILE), :]
    for n in range(GHOST):
        even, odd = even_ref[pl.ds(n * count, count), :], odd_ref[pl.ds(n * count, count), :]
        planes[pl.ds(n * count, count), :] = jnp.where(place.hi_odd, odd, even)
        planes[pl.ds((TILE - GHOST + n) * count, count), :] = jnp.where(place.hi_odd, even, odd)
    for n in range(GHOST, TILE - GHOST):
        planes[pl.ds(n * count, count), :] = jnp.zeros((count, plan.ny), jnp.float32)
    first = (1 - place.hi // 2) * count
    for n in range(count):
        ghost[rows_at(first + n), :] = planes[pl.ds(n, TILE, stride=count), :]
    deep, tiles = GHOST - 1, plan.z_tiles
    for side, (raw, z_send) in enumerate(zip(raws, z_sends)):
        up = jnp.logical_not(place.zb_odd) if side == 0 else place.zb_odd
        for t in range(plan.steps):
            for n in range(GHOST):
                e = GHOST + jnp.where(up, plan.nz - GHOST + n, n)
                for k in range(plan.main):
                    to = rows_at(t * tiles + n * plan.main + k)
                    z_send[to, :] = source[rows_at((e * plan.tiles + k) * plan.steps + t), :]
            for n in range(deep):
                z = t * plan.nz + jnp.where(up, plan.nz - deep + n, n)
                z_send[rows_at(t * tiles + GHOST * plan.main + n), :] = ghost[rows_at(z), :]
        z_send[rows_at(plan.steps * tiles, plan.raw_tiles), :] = raw[...]


class Sweeps:
    def __init__(self, plan, place, coefs, source, ping, pong, last):
        self.plan, self.coefs = plan, coefs
        self.source, self.buffers, self.last = source, (ping, pong), last
        self.has_low, self.has_high = place.zb > 0, place.zb < plan.z_parts - 1
        self.low_at, self.high_at = GHOST, GHOST + plan.nz

    def spot(self, e, k, t):
        return rows_at((e * self.plan.tiles + k) * self.plan.steps + t)

    def coef(self, e, k, n):
        return self.coefs[rows_at((e * self.plan.tiles + k) * COEFS + n), :]

    def first(self, e, k, values, scaled=False):
        w, c, wrap = (self.coef(e, k, n) for n in range(3))
        partial = []
        for t, value in enumerate(values):
            value = value if scaled else w * value
            self.source[self.spot(e, k, t), :] = value
            if t:
                value = value + c * partial[-1]
            partial.append(value)
        carry = c * (wrap * partial[-1])
        for t, value in enumerate(partial):
            self.buffers[0][self.spot(e, k, t), :] = value + carry
            carry = c * carry

    def sweep(self, number, start, stop, total=None):
        plan, steps, tiles, ny = self.plan, self.plan.steps, self.plan.tiles, self.plan.ny
        old, new = self.buffers[(number - 1) % 2], self.buffers[number % 2]
        final = number == SWEEPS - 1
        wide = plan.main if final else tiles
        row = sublane(plan)
        spot, coef = self.spot, self.coef

        def layers(e, count):
            parts = [(e + g, k) for g in range(count) for k in range(wide)]
            c = [coef(at, k, 1) for at, k in parts]
            near = [[coef(at, k, n) for n in range(3, COEFS)] for at, k in parts]
            partial = [[] for _ in parts]
            for g in range(count):
                at = e + g
                for t in range(steps):
                    here = [old[spot(at, k, t), :] for k in range(tiles)]
                    down = [pltpu.roll(value, 1, 0) for value in here]
                    up = [pltpu.roll(value, TILE - 1, 0) for value in here]
                    for k in range(wide):
                        n = g * wide + k
                        z_low, x_low, y_low, z_high, x_high, y_high = near[n]
                        below = jnp.where(row == 0, down[k - 1], down[k])
                        above = jnp.where(row == TILE - 1, up[(k + 1) % tiles], up[k])
                        total = self.source[spot(at, k, t), :] + z_low * old[spot(at - 1, k, t), :]
                        total = total + z_high * old[spot(at + 1, k, t), :]
                        total = total + (x_low * below + x_high * above)
                        total = total + (
                            y_low * pltpu.roll(here[k], 1, 1) + y_high * pltpu.roll(here[k], ny - 1, 1)
                        )
                        if t:
                            total = total + c[n] * partial[n][-1]
                        partial[n].append(total)
            for n, (at, k) in enumerate(parts):
                carry = c[n] * (coef(at, k, 2) * partial[n][-1])
                for t in range(steps):
                    value = partial[n][t] + carry
                    carry = c[n] * carry
                    if final:
                        self.last[rows_at((t * plan.nz + at - GHOST) * plan.main + k), :] = value
                    else:
                        new[spot(at, k, t), :] = value

        if total is not None:

            def several(i, _):
                layers(start + i * GROUP, GROUP)
                return 0

            lax.fori_loop(0, total // GROUP, several, 0)
            if total % GROUP:
                layers(start + total // GROUP * GROUP, total % GROUP)
        else:

            def one(e, _):
                layers(e, 1)
                return 0

            lax.fori_loop(start, stop, one, 0)


def first_pass(plan, work, ghost, start, count):
    def layer(z):
        work.first(z + GHOST, plan.main, [ghost[rows_at(t * plan.nz + z), :] for t in range(plan.steps)])

    def several(i, _):
        for n in range(4):
            layer(start + i * 4 + n)
        return 0

    lax.fori_loop(0, count // 4, several, 0)
    for n in range(count // 4 * 4, count):
        layer(start + n)


def ghost_pass(plan, place, work, z_in):
    steps, main, sides, deep = plan.steps, plan.main, plan.sides, GHOST - 1
    coefs, source, ping = work.coefs, work.source, work.buffers[0]
    empty = jnp.zeros((TILE, plan.ny), jnp.float32)

    def ghost_layers(at, upper, z_ref):
        for n in range(GHOST):
            e = at + n
            for k in range(plan.tiles):
                raw = steps * plan.z_tiles + (n * plan.tiles + k) * RAW

                def store(number, value, k=k, e=e):
                    coefs[rows_at((e * plan.tiles + k) * COEFS + number), :] = value

                write_coefs(plan, place.hi, None, k, [z_ref[rows_at(raw + m), :] for m in range(RAW)], store)
            for k in range(main):
                tile = n * main + k
                work.first(e, k, [z_ref[rows_at(t * plan.z_tiles + tile), :] for t in range(steps)], True)
            c_at = n if upper else n - (GHOST - deep)
            if 0 <= c_at < deep:
                tile = GHOST * main + c_at
                work.first(e, main, [z_ref[rows_at(t * plan.z_tiles + tile), :] for t in range(steps)])
            else:
                for t in range(steps):
                    ping[work.spot(e, main, t), :] = empty
                    source[work.spot(e, main, t), :] = empty

    for odd in (False, True):

        @pl.when(work.has_low & (place.zb_odd == odd))
        def _(odd=odd):
            ghost_layers(0, False, z_in[0 if odd else sides - 1])

        @pl.when(work.has_high & (place.zb_odd == odd))
        def _(odd=odd):
            ghost_layers(work.high_at, True, z_in[sides - 1 if odd else 0])


def no_ghosts(plan, work):
    empty = jnp.zeros((TILE, plan.ny), jnp.float32)
    for outside, e in ((work.has_low, work.low_at - 1), (work.has_high, work.high_at)):

        @pl.when(jnp.logical_not(outside))
        def _(e=e):
            for k in range(plan.tiles):
                for t in range(plan.steps):
                    for buffer in work.buffers:
                        buffer[work.spot(e, k, t), :] = empty


def write_piece(plan, place, last, outs, number):
    for out, (r, piece) in zip(outs, plan.back[number]):
        start = 0 if piece is None else place.piece(plan, piece)
        at = ((place.t ^ r) * plan.nz + start) * plan.rows
        out[...] = last[pl.ds(pl.multiple_of(at, TILE), out.shape[0]), :]


def all_sweeps(plan, place_ref, coefs_in, source_in, ping_in, ghost, *refs):
    place = Place(plan, place_ref)
    z_in, refs = refs[: plan.sides], refs[plan.sides :]
    outs, (coefs, source, ping, pong, last) = refs[:-5], refs[-5:]
    work = Sweeps(plan, place, coefs, source, ping, pong, last)
    first_pass(plan, work, ghost, 0, plan.nz)
    ghost_pass(plan, place, work, z_in)
    no_ghosts(plan, work)
    for number in range(1, SWEEPS):
        reach = SWEEPS - 1 - number
        start = work.low_at - jnp.where(work.has_low, reach, 0)
        stop = work.high_at + jnp.where(work.has_high, reach, 0)
        work.sweep(number, start, stop)
    write_piece(plan, place, last, outs, 0)


def far_sweeps(plan, place_ref, coefs, source_in, ping_in, *refs):
    place = Place(plan, place_ref)
    given, refs = refs[: plan.ghost_inputs], refs[plan.ghost_inputs :]
    outs, (source, ping, pong, last, ghost, z_send, planes) = refs[:-7], refs[-7:]
    gather_ghosts(plan, place_ref, source, *given, ghost, z_send, planes)
    work = Sweeps(plan, place, coefs, source, ping, pong, last)
    count = plan.pieces()[0]
    first_pass(plan, work, ghost, jnp.where(place.up, 0, plan.nz - count - GHOST), count + GHOST)
    no_ghosts(plan, work)
    for number in range(1, SWEEPS):
        total = count + SWEEPS - 1 - number
        start = jnp.where(place.up, work.low_at, work.high_at - total)
        work.sweep(number, start, start + total, total)
    write_piece(plan, place, last, outs, 0)


def near_sweeps(plan, place_ref, ghost, z_in, coefs_in, source_in, ping_in, pong_in, last_in, *refs):
    place = Place(plan, place_ref)
    outs, (coefs, source, ping, pong, last) = refs[:-5], refs[-5:]
    work = Sweeps(plan, place, coefs, source, ping, pong, last)
    first, count = plan.pieces()
    left = plan.nz - first - GHOST
    first_pass(plan, work, ghost, jnp.where(place.up, plan.nz - left, 0), left)
    ghost_pass(plan, place, work, [z_in])
    for number in range(1, SWEEPS):
        reach = SWEEPS - 1 - number
        start = jnp.where(place.up, work.low_at + first + reach, work.low_at - reach)
        work.sweep(number, start, start + count, count)
    write_piece(plan, place, last, outs, 1)


def run_sweeps(plan, call, coefs, source, ping, ghost_inputs):
    steps, ny = plan.steps, plan.ny
    grid = (plan.ext * plan.tiles * steps * TILE, ny)
    whole = (steps * plan.nz * plan.rows, ny)
    ghost = (steps * plan.nz * TILE, ny)
    z_send = ((steps * plan.z_tiles + plan.raw_tiles) * TILE, ny)
    planes = pltpu.VMEM((steps // 2 * plan.nz * TILE, ny), jnp.float32)
    shapes = [[(plan.layers(piece) * plan.rows, ny) for r, piece in blocks] for blocks in plan.back]

    def along_z(sends):
        return [lax.ppermute(send, FLAT, plan.z_pairs(first)) for first, send in enumerate(sends)]

    if len(shapes) == 1:
        ghost, *z_sends = call(
            gather_ghosts, [ghost] + [z_send] * plan.sides, (source, *ghost_inputs), scratch=[planes]
        )
        found = call(
            all_sweeps,
            shapes[0] + [coefs.shape, grid, grid],
            (coefs, source, ping, ghost, *along_z(z_sends)),
            scratch=[pltpu.VMEM(shape, jnp.float32) for shape in (grid, whole)],
            aliases={1 + n: len(shapes[0]) + n for n in range(3)},
            limit=24,
        )
        return [found[:-3]]
    *done, source, ping, pong, last, ghost, z_send = call(
        far_sweeps,
        shapes[0] + [grid] * 3 + [whole, ghost, z_send],
        (coefs, source, ping, *ghost_inputs),
        scratch=[planes],
        aliases={2 + n: len(shapes[0]) + n for n in range(2)},
        limit=24,
    )
    rest = call(
        near_sweeps,
        shapes[1] + [coefs.shape] + [grid] * 3 + [whole],
        (ghost, *along_z([z_send]), coefs, source, ping, pong, last),
        aliases={3 + n: len(shapes[1]) + n for n in range(5)},
        limit=24,
    )
    return [done, rest[:-5]]


def place_blocks(plan, listed, place_ref, *refs):
    place = Place(plan, place_ref)
    blocks, (out, sems) = refs[: len(listed)], refs[-2:]
    copies = []
    for n, (block, (r, piece)) in enumerate(zip(blocks, listed)):
        source = place.t ^ r
        quarter, lo = source // plan.per_quarter, source % plan.per_quarter
        z = lo // 2 * plan.nz + (0 if piece is None else place.piece(plan, piece))
        x = pl.multiple_of(quarter * plan.rows, plan.rows)
        target = out.at[lo % 2, pl.ds(z, plan.layers(piece)), pl.ds(x, plan.rows), :]
        copies.append(pltpu.make_async_copy(block, target, sems.at[n]))
    for copy in copies:
        copy.start()
    for copy in copies:
        copy.wait()


def local(right_side, diffusivity, velocity):
    steps, cores = lax.axis_size("tm"), lax.axis_size("space")
    _, parts, half_z, nx, ny = right_side.shape
    plan = Plan(steps, cores, half_z, nx, ny)
    place = jnp.stack([lax.axis_index("tm"), lax.axis_index("space")]).astype(jnp.int32)
    size = plan.nz * plan.rows
    half_x = steps // 2 * plan.nz

    def call(body, outs, arrays, extra=None, **options):
        body = functools.partial(body, plan) if extra is None else functools.partial(body, plan, extra)
        return kernel_call(body, outs, (place, *arrays), **options)

    def turned(arrays, rounds, ties=(), known=()):
        found = list(known)
        for n, (array, r) in enumerate(zip(arrays, rounds), len(found)):
            for late, early in ties:
                if n == late:
                    array, found[early] = lax.optimization_barrier((array, found[early]))
            found.append(array if r == 0 else lax.ppermute(array, "tm", plan.pairs(r)))
        return found

    sends = call(
        pack_blocks,
        [(plan.nz * plan.stride(r), ny) for r in plan.rounds],
        (right_side.reshape(parts * half_z * nx, ny),),
        extra=plan.rounds,
    )
    blocks = turned(sends, plan.rounds)
    blocks = lax.optimization_barrier(blocks)
    x_even, x_odd = call(edge_rows, [(GHOST * half_x, ny)] * 2, blocks)
    even = lax.ppermute(x_even, "tm", plan.x_pairs(0))
    odd = lax.ppermute(x_odd, "tm", plan.x_pairs(1))
    diffusivity, velocity, *blocks = lax.optimization_barrier((diffusivity, velocity, *blocks))
    coefs, *raws = call(
        make_coefs,
        [(plan.ext * plan.tiles * COEFS * TILE, ny)] + [(plan.raw_tiles * TILE, ny)] * plan.sides,
        (diffusivity.reshape(half_z * nx, ny), velocity.reshape(3 * half_z * nx, ny)),
    )
    direct = [block for block, r in zip(blocks, plan.rounds) if plan.direct(r)]
    grid = (plan.ext * plan.tiles * steps * TILE, ny)
    source, ping = call(
        first_own, [grid, grid], (coefs, *blocks), scratch=[pltpu.VMEM((steps * size, ny), jnp.float32)]
    )
    solved = run_sweeps(plan, call, coefs, source, ping, (even, odd, *direct, *raws))
    back = []
    for found, blocks in zip(solved, plan.back):
        back = turned(found, [r for r, piece in blocks], plan.ties, back)
    back = [
        block.reshape(plan.layers(piece), plan.rows, ny) for block, (r, piece) in zip(back, sum(plan.back, []))
    ]
    listed = sum(plan.back, [])
    cut = EARLY if len(plan.back) == 2 else 0
    begun = []
    for chosen in (range(cut), range(cut, len(back))):
        if len(chosen):
            out = call(
                place_blocks,
                (parts, half_z, nx, ny),
                [back[n] for n in chosen] + begun,
                extra=[listed[n] for n in chosen],
                spaces=[pltpu.VMEM] * len(chosen) + [pltpu.HBM] * len(begun),
                scratch=[pltpu.SemaphoreType.DMA((len(chosen),))],
                out_space=pltpu.HBM,
                aliases={1 + len(chosen): 0} if begun else None,
            )
            begun = [out]
    return out[None]


def solution(mesh):
    placed = (
        P(("group", "tm"), None, "space", None, None),
        P("space", None, None),
        P(None, "space", None, None),
    )
    return jax.shard_map(
        local,
        mesh=mesh,
        in_specs=placed,
        out_specs=P(("group", "tm"), None, "space", None, None),
        check_vma=False,
    )
```
